32 devices in a mesh: tensor: 2 (over x), context: 4 (over y, core), fsdp: 4 (over z).
Axes of the slice: x: 2, y: 2, z: 4, core: 2. Of those that a mesh axis runs over, the one named last changes fastest.
Arguments:
- tokens: bfloat16 [4, 1024, 2048], P('fsdp', 'context'), may hold values from -6 to 6
- segments: int32 [4, 1024], P('fsdp'), may hold values from 0 to 7, as said below
- positions: int32 [4, 1024], P('fsdp', 'context'), may hold values from 0 to 511, as said below
- attn_gain: bfloat16 [2048], P('fsdp'), may hold values from 0.099609375 to 1.8984375
- w_query: bfloat16 [2048, 2048], P('fsdp', 'tensor'), may hold values from -0.125 to 0.125
- w_key: bfloat16 [2048, 1024], P('fsdp', 'tensor'), may hold values from -0.125 to 0.125
- w_value: bfloat16 [2048, 1024], P('fsdp', 'tensor'), may hold values from -0.125 to 0.125
- w_out: bfloat16 [2048, 2048], P(('tensor', 'fsdp')), may hold values from -0.5 to 0.5
- ffn_gain: bfloat16 [2048], P('fsdp'), may hold values from 0.099609375 to 1.8984375
- w_gate: bfloat16 [2048, 8192], P('fsdp', 'tensor'), may hold values from -0.125 to 0.125
- w_up: bfloat16 [2048, 8192], P('fsdp', 'tensor'), may hold values from -0.125 to 0.125
- w_down: bfloat16 [8192, 2048], P(('tensor', 'fsdp')), may hold values from -0.0625 to 0.0625
- cotangent: bfloat16 [4, 1024, 2048], P('fsdp', 'context'), may hold values from -6 to 6
Outputs:
- output: bfloat16 [4, 1024, 2048], P('fsdp', 'context')
- grad_tokens: bfloat16 [4, 1024, 2048], P('fsdp', 'context')
- grad_attn_gain: float32 [2048], P(('context', 'fsdp'))
- grad_w_query: float32 [2048, 2048], P(('context', 'fsdp'), 'tensor')
- grad_w_key: float32 [2048, 1024], P(('context', 'fsdp'), 'tensor')
- grad_w_value: float32 [2048, 1024], P(('context', 'fsdp'), 'tensor')
- grad_w_out: float32 [2048, 2048], P(('tensor', 'context', 'fsdp'))
- grad_ffn_gain: float32 [2048], P(('context', 'fsdp'))
- grad_w_gate: float32 [2048, 8192], P(('context', 'fsdp'), 'tensor')
- grad_w_up: float32 [2048, 8192], P(('context', 'fsdp'), 'tensor')
- grad_w_down: float32 [8192, 2048], P(('tensor', 'context', 'fsdp'))
The draws below stay inside these ranges and needn't reach their ends.
Inputs may be any that keep to these rules, and one draw needn't show every extreme that they name: `segments`: A token's document number within its sequence: never falls along the sequence; each sequence holds 8 documents, one of them 1024 // 2 tokens long. `positions`: A token's place within its document: 0 at a document's first token, rising by one along it.
All inputs are finite; a program needn't handle non-finite values.
Results may differ from the reference program's by a relative error of at most 0.014.
Values may be sent and summed in bfloat16 or wider, within the bound.
No kernel may reach another device: no remote copies, remote signals or barrier semaphores. Data moves between devices by JAX's collectives and lax.ppermute only.
A program may use at most 320 MiB of HBM per device.

```python
import math
import jax
import jax.numpy as jnp
from jax import lax

D = 2048
HEADS = 16
KV_HEADS = 8
HEAD = 128
FF = 8192
DOCS = 8
LEN = 1024
SEQS = 4


def document_layout(key):
    half_len = LEN // 2
    small_docs = DOCS - 1
    spare_rows = half_len - small_docs
    powers = jax.random.randint(jax.random.fold_in(key, 7), (SEQS, small_docs), 0, 7)
    weights = jnp.left_shift(jnp.ones_like(powers), powers)
    pieces = 1 + weights * spare_rows // jnp.sum(weights, axis=1, keepdims=True)
    remain = half_len - jnp.sum(pieces, axis=1)
    pieces = pieces.at[:, small_docs - 1].add(remain)
    lengths = jnp.concatenate([jnp.full((SEQS, 1), LEN - half_len, jnp.int32), pieces.astype(jnp.int32)], axis=1)
    order_keys = jax.random.split(jax.random.fold_in(key, 11), SEQS)
    orders = jax.vmap(lambda one_key: jax.random.permutation(one_key, DOCS))(order_keys)
    shuffled = jnp.take_along_axis(lengths, orders, axis=1)
    doc_ends = jnp.cumsum(shuffled, axis=1).astype(jnp.int32)
    starts = doc_ends - shuffled
    places = jnp.arange(LEN, dtype=jnp.int32)
    documents = jnp.sum((places[None, :, None] >= doc_ends[:, None, :]).astype(jnp.int32), axis=2).astype(jnp.int32)
    first_place = jnp.take_along_axis(starts, documents, axis=1)
    return (documents, (places[None, :] - first_place).astype(jnp.int32))


def draw_segments(key, part):
    return document_layout(key)[0]


def draw_positions(key, part):
    return document_layout(key)[1]


def block_levels(stream_key, extent, cuts, low, largest):
    level, own = 1.0, jax.random.fold_in(stream_key, 6)
    for axis_at, shards_of in cuts:
        draws = jnp.exp(jax.random.uniform(jax.random.fold_in(own, axis_at), (shards_of,), jnp.float32, low / len(cuts), largest / len(cuts)))
        level = level * jnp.repeat(draws, extent[axis_at] // shards_of).reshape([-1 if axis == axis_at else 1 for axis in range(len(extent))])
    return level


def gaussian(stream_key, dims, width, limit, cuts=(), kind=jnp.bfloat16):
    level = block_levels(stream_key, dims, cuts, -0.22, 0.18) if cuts else 1.0
    entries = jax.random.normal(stream_key, dims, jnp.float32) * width * level
    return jnp.minimum(jnp.maximum(entries, -limit), limit).astype(kind)


def setup_inputs(seed: int = 0) -> dict:
    seeds = jax.random.split(jax.random.key(seed), 14)
    tokens = gaussian(seeds[0], (SEQS, LEN, D), 1.0, 6.0, ((0, 4), (1, 4)))
    segments = draw_segments(jax.random.fold_in(seeds[13], 71), 0)
    positions = draw_positions(jax.random.fold_in(seeds[13], 71), 0)
    attn_gain = jnp.clip(1.0 + 0.18 * jax.random.normal(seeds[3], (D,), jnp.float32), 0.099609375, 1.8984375).astype(jnp.bfloat16)
    w_query = gaussian(seeds[4], (D, HEADS * HEAD), D ** -0.5, 0.125, ((0, 4), (1, 2)))
    w_key = gaussian(seeds[5], (D, KV_HEADS * HEAD), D ** -0.5, 0.125, ((0, 4), (1, 2)))
    w_value = gaussian(seeds[6], (D, KV_HEADS * HEAD), D ** -0.5, 0.125, ((0, 4), (1, 2)))
    w_out = gaussian(seeds[7], (HEADS * HEAD, D), (D // 16) ** -0.5, 0.5, ((0, 8),))
    ffn_gain = jnp.clip(1.0 + 0.18 * jax.random.normal(seeds[8], (D,), jnp.float32), 0.099609375, 1.8984375).astype(jnp.bfloat16)
    w_gate = gaussian(seeds[9], (D, FF), D ** -0.5, 0.125, ((0, 4), (1, 2)))
    w_up = gaussian(seeds[10], (D, FF), D ** -0.5, 0.125, ((0, 4), (1, 2)))
    w_down = gaussian(seeds[11], (FF, D), FF ** -0.5, 0.0625, ((0, 8),))
    cotangent = gaussian(seeds[12], (SEQS, LEN, D), 1.0, 6.0, ((0, 4), (1, 4)))
    return {"tokens": tokens, "segments": segments, "positions": positions, "attn_gain": attn_gain, "w_query": w_query, "w_key": w_key, "w_value": w_value, "w_out": w_out, "ffn_gain": ffn_gain, "w_gate": w_gate, "w_up": w_up, "w_down": w_down, "cotangent": cotangent}


norm_epsilon = 1e-05
rope_base = 1000000.0

@jax.custom_vjp
def low(v):
    return lax.optimization_barrier(v.astype(jnp.bfloat16)).astype(jnp.float32)

@jax.custom_vjp
def low_back(v):
    return v

def low_keep(v):
    return (low(v), None)

def low_pass(kept, grad):
    return (grad,)

def back_keep(v):
    return (v, None)

def back_low(kept, grad):
    return (low(grad),)
low.defvjp(low_keep, low_pass)
low_back.defvjp(back_keep, back_low)

def product(left, right):
    return jnp.dot(left, right, precision=lax.Precision.HIGHEST, preferred_element_type=jnp.float32)

def rotary(positions):
    freq_index = jnp.arange(HEAD // 2, dtype=jnp.float32)
    inverse = rope_base ** (-2.0 * freq_index / HEAD)
    angles = positions.astype(jnp.float32)[:, None] * inverse[None, :]
    angles = jnp.concatenate([angles, angles], axis=1)
    return (jnp.cos(angles), jnp.sin(angles))

def rotate(values, cos_table, sine_table):
    half_size = values.shape[-1] // 2
    lower_half = values[..., :half_size]
    upper_half = values[..., half_size:]
    turned = jnp.concatenate([-upper_half, lower_half], axis=-1)
    return values * cos_table[:, None, :] + turned * sine_table[:, None, :]

def norm_apply(values, gain):
    inverse_rms = lax.rsqrt(lax.optimization_barrier(jnp.mean(values * values, axis=-1, keepdims=True)) + norm_epsilon)
    return values * inverse_rms * gain

def attend_sequence(pieces):
    queries, key_rows, value_rows, seg_row = pieces
    length = queries.shape[0]
    block_rows = math.gcd(length, 512)
    block_count = length // block_rows
    key_order = jnp.arange(length, dtype=jnp.int32)
    score_scale = 1.0 / math.sqrt(HEAD)

    def one_block(parts):
        query_blk, seg_blk, order_blk = parts
        scores = jnp.einsum('qhgd,khd->hgqk', query_blk, key_rows, precision=lax.Precision.HIGHEST) * score_scale
        scores = low_back(scores)
        allowed = (seg_blk[:, None] == seg_row[None, :]) & (order_blk[:, None] >= key_order[None, :])
        scores = jnp.where(allowed[None, None], scores, -1e+30)
        probabilities = low(jax.nn.softmax(scores, axis=-1))
        return jnp.einsum('hgqk,khd->qhgd', probabilities, value_rows, precision=lax.Precision.HIGHEST)
    stacked = (queries.reshape((block_count, block_rows) + queries.shape[1:]), seg_row.reshape(block_count, block_rows), key_order.reshape(block_count, block_rows))
    attended = lax.map(jax.checkpoint(one_block), stacked)
    return attended.reshape(queries.shape)

def forward(residual, attn_gain, w_query, w_key, w_value, w_out, ffn_gain, w_gate, w_up, w_down, segments, positions):
    seq_count, length, model_width = residual.shape
    flat_rows = residual.reshape(seq_count * length, model_width)
    normed_one = low(norm_apply(flat_rows, attn_gain))
    query_raw = low_back(product(normed_one, w_query)).reshape(seq_count, length, HEADS, HEAD)
    key_raw = low_back(product(normed_one, w_key)).reshape(seq_count, length, KV_HEADS, HEAD)
    value_raw = low_back(product(normed_one, w_value)).reshape(seq_count, length, KV_HEADS, HEAD)
    cos_table, sine_table = jax.vmap(rotary)(positions)
    queries = low(jax.vmap(rotate)(query_raw, cos_table, sine_table))
    queries = queries.reshape(seq_count, length, KV_HEADS, HEADS // KV_HEADS, HEAD)
    key_rows = low(jax.vmap(rotate)(key_raw, cos_table, sine_table))
    value_rows = low(value_raw)
    attended = lax.map(jax.checkpoint(attend_sequence), (queries, key_rows, value_rows, segments))
    attended = low(low_back(attended)).reshape(seq_count * length, HEADS * HEAD)
    hidden = flat_rows + low_back(product(attended, w_out))
    normed_two = low(norm_apply(hidden, ffn_gain))
    gate_proj = low_back(product(normed_two, w_gate))
    up_proj = low_back(product(normed_two, w_up))
    activation = low(jax.nn.silu(gate_proj) * up_proj)
    block_out = hidden + low_back(product(activation, w_down))
    return block_out.reshape(seq_count, length, model_width)

def reference(tokens, segments, positions, attn_gain, w_query, w_key, w_value, w_out, ffn_gain, w_gate, w_up, w_down, cotangent):
    floats = [member.astype(jnp.float32) for member in (tokens, attn_gain, w_query, w_key, w_value, w_out, ffn_gain, w_gate, w_up, w_down)]

    def wrapped(*values):
        return forward(*values, segments, positions)
    block_out, pullback = jax.vjp(wrapped, *floats)
    gradients = pullback(cotangent.astype(jnp.float32))
    return (block_out.astype(jnp.bfloat16), gradients[0].astype(jnp.bfloat16), gradients[1], gradients[2], gradients[3], gradients[4], gradients[5], gradients[6], gradients[7], gradients[8], gradients[9])
```

```python
import math

import jax
import jax.numpy as jnp
from jax import lax
from jax.sharding import PartitionSpec as P

HEAD = 128


norm_epsilon = 1e-05
rope_base = 1000000.0


def rotary(positions):
    freq_index = jnp.arange(HEAD // 2, dtype=jnp.float32)
    inverse = rope_base ** (-2.0 * freq_index / HEAD)
    angles = positions.astype(jnp.float32)[:, None] * inverse[None, :]
    angles = jnp.concatenate([angles, angles], axis=1)
    return (jnp.cos(angles), jnp.sin(angles))


def rotate(values, cos_table, sine_table):
    half_size = values.shape[-1] // 2
    lower_half = values[..., :half_size]
    upper_half = values[..., half_size:]
    turned = jnp.concatenate([-upper_half, lower_half], axis=-1)
    return values * cos_table[:, None, :] + turned * sine_table[:, None, :]


def unrotate(grad_rot, cos_table, sine_table):
    half_size = grad_rot.shape[-1] // 2
    scaled = grad_rot * sine_table[:, None, :]
    swapped = jnp.concatenate([scaled[..., half_size:], -scaled[..., :half_size]], axis=-1)
    return grad_rot * cos_table[:, None, :] + swapped


def norm_forward(values):
    inverse_rms = lax.rsqrt(jnp.mean(values * values, axis=-1, keepdims=True) + norm_epsilon)
    return (inverse_rms, values * inverse_rms)


def norm_backward(grad_normed, gain, inverse_rms, normalized):
    scaled = grad_normed * gain
    return inverse_rms * (
        scaled - normalized * jnp.mean(scaled * normalized, axis=-1, keepdims=True)
    )


def contract_rows(left, right):
    return lax.dot_general(
        left, right, (((0,), (0,)), ((), ())), preferred_element_type=jnp.float32
    )


def contract_cols(left, right):
    return lax.dot_general(
        left, right, (((1,), (1,)), ((), ())), preferred_element_type=jnp.float32
    )


def block_scores(query_blk, key_all, query_seg, key_seg, query_order, key_order, score_scale):
    scores = (
        jnp.einsum("qhgd,khd->hgqk", query_blk, key_all, preferred_element_type=jnp.float32)
        * score_scale
    )
    allowed = (query_seg[:, None] == key_seg[None, :]) & (
        query_order[:, None] >= key_order[None, :]
    )
    return jnp.where(allowed[None, None], scores, -1e30)


def attend_forward(
    queries, key_all, value_all, query_seg, key_seg, query_order, key_order, block_rows, score_scale
):
    block_count = queries.shape[0] // block_rows

    def one_block(pieces):
        query_blk, seg_blk, order_blk = pieces
        scores = block_scores(
            query_blk, key_all, seg_blk, key_seg, order_blk, key_order, score_scale
        )
        highest = jnp.max(scores, axis=-1, keepdims=True)
        weights = jnp.exp(scores - highest)
        row_total = jnp.sum(weights, axis=-1, keepdims=True)
        probabilities = weights / row_total
        attended = jnp.einsum(
            "hgqk,khd->qhgd",
            probabilities.astype(jnp.bfloat16),
            value_all,
            preferred_element_type=jnp.float32,
        )
        return (attended, highest + jnp.log(row_total))

    stacked = (
        queries.reshape((block_count, block_rows) + queries.shape[1:]),
        query_seg.reshape(block_count, block_rows),
        query_order.reshape(block_count, block_rows),
    )
    attended, logsum = lax.map(one_block, stacked)
    return (attended.reshape(queries.shape), logsum)


def attend_backward(
    queries,
    key_all,
    value_all,
    grad_attended,
    logsum,
    query_seg,
    key_seg,
    query_order,
    key_order,
    block_rows,
    score_scale,
):
    block_count = queries.shape[0] // block_rows
    empty_grad = jnp.zeros(key_all.shape, jnp.float32)

    def one_block(carry, pieces):
        grad_key, grad_value = carry
        query_blk, grad_blk, logsum_blk, seg_blk, order_blk = pieces
        scores = block_scores(
            query_blk, key_all, seg_blk, key_seg, order_blk, key_order, score_scale
        )
        probabilities = jnp.exp(scores - logsum_blk)
        grad_probs = jnp.einsum(
            "qhgd,khd->hgqk", grad_blk, value_all, preferred_element_type=jnp.float32
        )
        row_delta = jnp.sum(probabilities * grad_probs, axis=-1, keepdims=True)
        grad_scores = (probabilities * (grad_probs - row_delta)).astype(jnp.bfloat16)
        grad_query = score_scale * jnp.einsum(
            "hgqk,khd->qhgd", grad_scores, key_all, preferred_element_type=jnp.float32
        )
        grad_key = grad_key + score_scale * jnp.einsum(
            "hgqk,qhgd->khd", grad_scores, query_blk, preferred_element_type=jnp.float32
        )
        grad_value = grad_value + jnp.einsum(
            "hgqk,qhgd->khd",
            probabilities.astype(jnp.bfloat16),
            grad_blk,
            preferred_element_type=jnp.float32,
        )
        return ((grad_key, grad_value), grad_query)

    stacked = (
        queries.reshape((block_count, block_rows) + queries.shape[1:]),
        grad_attended.reshape((block_count, block_rows) + grad_attended.shape[1:]),
        logsum,
        query_seg.reshape(block_count, block_rows),
        query_order.reshape(block_count, block_rows),
    )
    (grad_key, grad_value), grad_query = lax.scan(one_block, (empty_grad, empty_grad), stacked)
    return (grad_query.reshape(queries.shape), grad_key, grad_value)


def per_device_general(
    tokens,
    segments,
    positions,
    attn_gain,
    w_query,
    w_key,
    w_value,
    w_out,
    ffn_gain,
    w_gate,
    w_up,
    w_down,
    cotangent,
):
    token_count = tokens.shape[1]
    residual = tokens[0].astype(jnp.float32)
    seq_start = lax.axis_index("context") * token_count
    key_seg = segments[0]
    key_order = jnp.arange(key_seg.shape[0], dtype=jnp.int32)
    query_seg = lax.dynamic_slice_in_dim(key_seg, seq_start, token_count)
    query_order = seq_start + jnp.arange(token_count, dtype=jnp.int32)
    cos_table, sine_table = rotary(positions[0])
    block_rows = math.gcd(token_count, 512)
    score_scale = 1.0 / math.sqrt(HEAD)
    gain_one, query_w, key_w, value_w, out_w = (
        lax.all_gather(attn_gain, "fsdp", axis=0, tiled=True),
        lax.all_gather(w_query, "fsdp", axis=0, tiled=True),
        lax.all_gather(w_key, "fsdp", axis=0, tiled=True),
        lax.all_gather(w_value, "fsdp", axis=0, tiled=True),
        lax.all_gather(w_out, "fsdp", axis=0, tiled=True),
    )
    gain_two, gate_w, up_w, down_w = (
        lax.all_gather(ffn_gain, "fsdp", axis=0, tiled=True),
        lax.all_gather(w_gate, "fsdp", axis=0, tiled=True),
        lax.all_gather(w_up, "fsdp", axis=0, tiled=True),
        lax.all_gather(w_down, "fsdp", axis=0, tiled=True),
    )
    query_heads = query_w.shape[1] // HEAD
    kv_heads = key_w.shape[1] // HEAD
    group_size = query_heads // kv_heads
    inverse_one, normal_one = norm_forward(residual)
    normed_one = (normal_one * gain_one.astype(jnp.float32)).astype(jnp.bfloat16)
    query_raw = jnp.dot(normed_one, query_w, preferred_element_type=jnp.float32)
    key_raw = jnp.dot(normed_one, key_w, preferred_element_type=jnp.float32)
    value_raw = jnp.dot(normed_one, value_w, preferred_element_type=jnp.float32)
    queries = rotate(
        query_raw.reshape(token_count, query_heads, HEAD), cos_table, sine_table
    ).astype(jnp.bfloat16)
    queries = queries.reshape(token_count, kv_heads, group_size, HEAD)
    key_local = rotate(key_raw.reshape(token_count, kv_heads, HEAD), cos_table, sine_table).astype(
        jnp.bfloat16
    )
    value_local = value_raw.astype(jnp.bfloat16).reshape(token_count, kv_heads, HEAD)
    key_all, value_all = (
        lax.all_gather(key_local, "context", axis=0, tiled=True),
        lax.all_gather(value_local, "context", axis=0, tiled=True),
    )
    attended, logsum = attend_forward(
        queries,
        key_all,
        value_all,
        query_seg,
        key_seg,
        query_order,
        key_order,
        block_rows,
        score_scale,
    )
    attended_low = attended.reshape(token_count, query_heads * HEAD).astype(jnp.bfloat16)
    attn_part = jnp.dot(attended_low, out_w, preferred_element_type=jnp.float32)
    hidden = residual + lax.psum(attn_part, "tensor")
    inverse_two, normal_two = norm_forward(hidden)
    normed_two = (normal_two * gain_two.astype(jnp.float32)).astype(jnp.bfloat16)
    gate_proj = jnp.dot(normed_two, gate_w, preferred_element_type=jnp.float32)
    up_proj = jnp.dot(normed_two, up_w, preferred_element_type=jnp.float32)
    sigmoid_gate = jax.nn.sigmoid(gate_proj)
    silu_gate = gate_proj * sigmoid_gate
    activation = (silu_gate * up_proj).astype(jnp.bfloat16)
    ffn_part = jnp.dot(activation, down_w, preferred_element_type=jnp.float32)
    block_out = hidden + lax.psum(ffn_part.astype(jnp.bfloat16), "tensor").astype(jnp.float32)
    output = block_out.astype(jnp.bfloat16)[None]
    grad_rows = cotangent[0]
    term_down = contract_rows(activation, grad_rows)
    grad_act = contract_cols(grad_rows, down_w)
    grad_gate = (
        grad_act * up_proj * sigmoid_gate * (1.0 + gate_proj * (1.0 - sigmoid_gate))
    ).astype(jnp.bfloat16)
    grad_up = (grad_act * silu_gate).astype(jnp.bfloat16)
    term_gate = contract_rows(normed_two, grad_gate)
    term_up = contract_rows(normed_two, grad_up)
    grad_norm_two = contract_cols(grad_gate, gate_w) + contract_cols(grad_up, up_w)
    grad_norm_two = lax.psum(grad_norm_two, "tensor")
    term_gain_two = jnp.sum(grad_norm_two * normal_two, axis=0)
    grad_hidden = grad_rows.astype(jnp.float32) + norm_backward(
        grad_norm_two, gain_two.astype(jnp.float32), inverse_two, normal_two
    )
    hidden_low = grad_hidden.astype(jnp.bfloat16)
    term_out = contract_rows(attended_low, hidden_low)
    grad_attended = (
        contract_cols(hidden_low, out_w)
        .astype(jnp.bfloat16)
        .reshape(token_count, kv_heads, group_size, HEAD)
    )
    key_back, value_back = (key_all, value_all)
    grad_query, grad_key_all, grad_value_all = attend_backward(
        queries,
        key_back,
        value_back,
        grad_attended,
        logsum,
        query_seg,
        key_seg,
        query_order,
        key_order,
        block_rows,
        score_scale,
    )
    grad_key_rot, grad_value_rot = (
        lax.psum_scatter(grad_key_all, "context", scatter_dimension=0, tiled=True),
        lax.psum_scatter(grad_value_all, "context", scatter_dimension=0, tiled=True),
    )
    grad_query_low = unrotate(
        grad_query.reshape(token_count, query_heads, HEAD), cos_table, sine_table
    )
    grad_query_low = grad_query_low.reshape(token_count, query_heads * HEAD).astype(jnp.bfloat16)
    grad_key_low = (
        unrotate(grad_key_rot, cos_table, sine_table)
        .reshape(token_count, kv_heads * HEAD)
        .astype(jnp.bfloat16)
    )
    grad_value_low = grad_value_rot.reshape(token_count, kv_heads * HEAD).astype(jnp.bfloat16)
    term_query = contract_rows(normed_one, grad_query_low)
    term_key = contract_rows(normed_one, grad_key_low)
    term_value = contract_rows(normed_one, grad_value_low)
    grad_norm_one = (
        contract_cols(grad_query_low, query_w)
        + contract_cols(grad_key_low, key_w)
        + contract_cols(grad_value_low, value_w)
    )
    grad_norm_one = lax.psum(grad_norm_one, "tensor")
    term_gain_one = jnp.sum(grad_norm_one * normal_one, axis=0)
    grad_input = grad_hidden + norm_backward(
        grad_norm_one, gain_one.astype(jnp.float32), inverse_one, normal_one
    )
    summed = (
        lax.psum_scatter(term_gain_one, ("context", "fsdp"), scatter_dimension=0, tiled=True),
        lax.psum_scatter(term_query, ("context", "fsdp"), scatter_dimension=0, tiled=True),
        lax.psum_scatter(term_key, ("context", "fsdp"), scatter_dimension=0, tiled=True),
        lax.psum_scatter(term_value, ("context", "fsdp"), scatter_dimension=0, tiled=True),
        lax.psum_scatter(term_out, ("context", "fsdp"), scatter_dimension=0, tiled=True),
        lax.psum_scatter(term_gain_two, ("context", "fsdp"), scatter_dimension=0, tiled=True),
        lax.psum_scatter(term_gate, ("context", "fsdp"), scatter_dimension=0, tiled=True),
        lax.psum_scatter(term_up, ("context", "fsdp"), scatter_dimension=0, tiled=True),
        lax.psum_scatter(term_down, ("context", "fsdp"), scatter_dimension=0, tiled=True),
    )
    return (
        output,
        grad_input.astype(jnp.bfloat16)[None],
        summed[0],
        summed[1],
        summed[2],
        summed[3],
        summed[4],
        summed[5],
        summed[6],
        summed[7],
        summed[8],
    )


def order_pair(mine, theirs, index):
    first = index == 0
    return jnp.stack([jnp.where(first, mine, theirs), jnp.where(first, theirs, mine)])


def pick(stack, index, axis=0):
    return lax.dynamic_index_in_dim(stack, index, axis, keepdims=False)


def over_core(block):
    return lax.ppermute(block, "context", [(i, i ^ 1) for i in range(4)])


def over_y(block):
    return lax.ppermute(block, "context", [(i, i ^ 2) for i in range(4)])


def over_diagonal(block):
    return lax.ppermute(block, "context", [(i, i ^ 3) for i in range(4)])


def over_x(block):
    return lax.ppermute(block, "tensor", [(0, 1), (1, 0)])


def shift_z(block, step):
    return lax.ppermute(block, "fsdp", [(i, (i + step) % 4) for i in range(4)])


def exchange_z(block, distance):
    return lax.ppermute(block, "fsdp", [(i, i ^ distance) for i in range(4)])


def ring_gather(block):
    blocks = [block]
    for _ in range(3):
        blocks.append(shift_z(blocks[-1], 1))
    return blocks


def ring_reduce(terms):
    total = terms[1]
    for step in (2, 3, 0):
        total = shift_z(total, 1).astype(jnp.float32) + terms[step].astype(jnp.float32)
        if step:
            total = total.astype(jnp.bfloat16)
    return total


def low(values):
    return values.astype(jnp.bfloat16)


def wide(values):
    return values.astype(jnp.float32)


def plane_reduce(partial):
    half = partial.shape[-1] // 2
    mine = low(wide(partial[0]) + wide(over_core(partial[1])))
    left, right = mine[..., :half], mine[..., half:]
    left = low(wide(left[:, 0]) + wide(over_x(left[:, 1])))
    right = low(wide(right[0]) + wide(over_y(right[1])))
    left = wide(left[0]) + wide(over_y(left[1]))
    right = wide(right[0]) + wide(over_x(right[1]))
    return jnp.concatenate([left, right], axis=-1)


def plane_gather(block):
    half = block.shape[-1] // 2
    left, right = block[:, :half], block[:, half:]
    left = jnp.stack([left, over_x(left)])
    right = jnp.stack([right, over_y(right)])
    left = jnp.stack([left, over_y(left)])
    right = jnp.stack([right, over_x(right)], axis=1)
    mine = jnp.concatenate([left, right], axis=-1)
    return jnp.stack([mine, over_core(mine)])


def group_spread(block):
    pair = jnp.stack([block, over_x(block)])
    return jnp.stack([pair, over_core(pair)])


def group_reduce(partial):
    mine = low(wide(partial[0]) + wide(over_core(partial[1])))
    return low(wide(mine[0]) + wide(over_x(mine[1])))


def gain_reduce(term, context_at, fsdp_at):
    y_at, core_at = context_at // 2, context_at % 2
    term = term + over_x(term)
    term = term.reshape(2, 2, 2, 2, -1)
    term = pick(term, core_at, 1) + over_core(pick(term, 1 - core_at, 1))
    term = pick(term, y_at) + over_y(pick(term, 1 - y_at))
    high, lowest = fsdp_at // 2, fsdp_at % 2
    term = pick(term, high) + exchange_z(pick(term, 1 - high), 2)
    return pick(term, lowest) + exchange_z(pick(term, 1 - lowest), 1)


def context_spread(blocks, context_at):
    got = jnp.stack(
        [
            pick(blocks, context_at),
            over_core(pick(blocks, context_at ^ 1)),
            over_y(pick(blocks, context_at ^ 2)),
            over_diagonal(pick(blocks, context_at ^ 3)),
        ]
    )
    return [pick(got, i ^ context_at) for i in range(4)]


def fsdp_spread(blocks, fsdp_at):
    got = [pick(blocks, fsdp_at)]
    for step in (1, 2, 3):
        got.append(shift_z(pick(blocks, (fsdp_at + step) % 4), step))
    got = jnp.stack(got)
    return [pick(got, (fsdp_at - i) % 4) for i in range(4)]


def attention_forward(queries, keys, values, allowed, score_scale):
    scores = jnp.einsum("qhd,kd->hqk", queries, keys, preferred_element_type=jnp.float32)
    scores = jnp.where(allowed[None], scores * score_scale, -1e30)
    highest = jnp.max(scores, axis=-1, keepdims=True)
    weights = jnp.exp(scores - highest)
    row_total = jnp.sum(weights, axis=-1, keepdims=True)
    probabilities = low(weights / row_total)
    attended = jnp.einsum(
        "hqk,kd->qhd", probabilities, values, preferred_element_type=jnp.float32
    )
    return low(attended), highest + jnp.log(row_total)


def attention_backward(queries, keys, values, grad_attended, logsum, allowed, score_scale):
    scores = jnp.einsum("qhd,kd->hqk", queries, keys, preferred_element_type=jnp.float32)
    scores = jnp.where(allowed[None], scores * score_scale, -1e30)
    probabilities = jnp.exp(scores - logsum)
    grad_probs = jnp.einsum(
        "qhd,kd->hqk", grad_attended, values, preferred_element_type=jnp.float32
    )
    row_delta = jnp.sum(probabilities * grad_probs, axis=-1, keepdims=True)
    grad_scores = low(probabilities * (grad_probs - row_delta))
    grad_query = score_scale * jnp.einsum(
        "hqk,kd->qhd", grad_scores, keys, preferred_element_type=jnp.float32
    )
    grad_key = score_scale * jnp.einsum(
        "hqk,qhd->kd", grad_scores, queries, preferred_element_type=jnp.float32
    )
    grad_value = jnp.einsum(
        "hqk,qhd->kd", low(probabilities), grad_attended, preferred_element_type=jnp.float32
    )
    return grad_query, grad_key, grad_value


def per_device_moved(
    tokens,
    segments,
    positions,
    attn_gain,
    w_query,
    w_key,
    w_value,
    w_out,
    ffn_gain,
    w_gate,
    w_up,
    w_down,
    cotangent,
):
    tensor_at, context_at, fsdp_at = (lax.axis_index(a) for a in ("tensor", "context", "fsdp"))
    y_at, core_at = context_at // 2, context_at % 2
    width = tokens.shape[2]
    block_rows = tokens.shape[1]
    rows = block_rows // 2
    length = segments.shape[1]
    score_scale = 1.0 / math.sqrt(HEAD)
    shard = attn_gain.shape[0]
    head_cols = w_query.shape[1] // 4
    kv_cols = w_key.shape[1] // 4
    group_size = head_cols // kv_cols

    def split_x(block):
        pair = block.reshape((2, rows) + block.shape[1:])
        return jnp.where(tensor_at == 0, pair, pair[::-1])

    def spread_context(block):
        pair = jnp.stack([block, over_y(block)])
        return jnp.stack([pair, over_core(pair)])

    own_tokens = split_x(tokens[0])
    all_tokens = spread_context(own_tokens)
    all_places = spread_context(split_x(positions[0])).reshape(length)

    def head_slice(weight, cols):
        return lax.dynamic_slice_in_dim(weight, context_at * cols, cols, axis=1)

    gains = jnp.zeros((16, head_cols + 2 * kv_cols), jnp.bfloat16)
    gains = gains.at[0, :shard].set(attn_gain).at[1, :shard].set(ffn_gain)
    packed = jnp.concatenate(
        [
            jnp.concatenate(
                [
                    head_slice(w_query, head_cols),
                    head_slice(w_key, kv_cols),
                    head_slice(w_value, kv_cols),
                ],
                axis=1,
            ),
            gains,
        ],
        axis=0,
    )
    packed_all = jnp.stack(ring_gather(packed))
    packed_all = jnp.stack([pick(packed_all, (fsdp_at - i) % 4) for i in range(4)])
    attn_w = packed_all[:, :shard].reshape(width, head_cols + 2 * kv_cols)
    gain_one = wide(packed_all[:, shard, :shard].reshape(width))
    gain_two = wide(packed_all[:, shard + 1, :shard].reshape(width))

    out_cols = w_out.shape[1] // 4
    out_part = lax.dynamic_slice_in_dim(w_out, context_at * out_cols, out_cols, axis=1)
    out_all = jnp.stack(ring_gather(out_part))
    out_all = jnp.stack([pick(out_all, (fsdp_at - i) % 4) for i in range(4)])
    out_w = jnp.concatenate(context_spread(out_all, context_at), axis=1)

    unit_half = w_gate.shape[1] // 16
    units = 2 * unit_half

    def unit_weights(weight):
        mine = weight.reshape(shard, 4, 2, 2, unit_half)
        mine = pick(pick(mine, core_at, 2), y_at, 2)
        return jnp.moveaxis(mine, 1, 0)

    both = jnp.stack([unit_weights(w_gate), unit_weights(w_up)], axis=1)
    both = jnp.stack(fsdp_spread(both, fsdp_at), axis=1).reshape(2, width, unit_half)
    both = order_pair(both, over_y(both), y_at)
    gate_w = jnp.concatenate([both[0, 0], both[1, 0]], axis=1)
    up_w = jnp.concatenate([both[0, 1], both[1, 1]], axis=1)
    down_w = lax.dynamic_slice_in_dim(w_down, core_at * units, units, axis=0)

    own_cotangent = split_x(cotangent[0])
    cotangent_ring = ring_gather(own_cotangent[0])
    cotangents = [jnp.stack([own_cotangent, over_core(own_cotangent)])] + [
        group_spread(block) for block in cotangent_ring[1:]
    ]
    cotangents = [block.reshape(4 * rows, width) for block in cotangents]

    def flip(block, axis, index):
        return jnp.where(index == 0, block, jnp.flip(block, axis))

    def relative(block):
        block = block.reshape(2, 2, 2, rows)
        block = flip(flip(flip(block, 0, y_at), 1, core_at), 2, tensor_at)
        return jnp.swapaxes(block, 0, 1).reshape(length)

    order = relative(jnp.arange(length, dtype=jnp.int32))
    seg = relative(segments[0])
    allowed = (seg[:, None] == seg[None, :]) & (order[:, None] >= order[None, :])
    cos_table, sine_table = rotary(all_places)
    residual = wide(all_tokens.reshape(length, width))
    inverse_one, normal_one = norm_forward(residual)
    normed_one = low(normal_one * gain_one)
    projected = jnp.dot(normed_one, attn_w, preferred_element_type=jnp.float32)
    heads = projected[:, : head_cols + kv_cols].reshape(length, group_size + 1, HEAD)
    turned = low(rotate(heads, cos_table, sine_table))
    queries, keys = turned[:, :group_size], turned[:, group_size]
    values = low(projected[:, head_cols + kv_cols :])
    attended, logsum = attention_forward(queries, keys, values, allowed, score_scale)
    attended = attended.reshape(length, head_cols)
    attn_part = low(jnp.dot(attended, out_w, preferred_element_type=jnp.float32))
    hidden = residual[:rows] + plane_reduce(attn_part.reshape(2, 2, 2, rows, width))
    inverse_two, normal_two = norm_forward(hidden)
    normed_two = low(normal_two * gain_two)

    kept = []
    out_terms, norm_terms = [None] * 4, [None] * 4
    ring = ring_gather(normed_two)
    for step in (0, 1, 2, 3):
        normed = group_spread(ring[step]).reshape(4 * rows, width)
        gate_proj = jnp.dot(normed, gate_w, preferred_element_type=jnp.float32)
        up_proj = jnp.dot(normed, up_w, preferred_element_type=jnp.float32)
        sigmoid_gate = jax.nn.sigmoid(gate_proj)
        silu_gate = gate_proj * sigmoid_gate
        activation = low(silu_gate * up_proj)
        grad_rows = cotangents[step]
        grad_act = contract_cols(grad_rows, down_w)
        grad_gate = low(grad_act * up_proj * sigmoid_gate * (1.0 + gate_proj * (1.0 - sigmoid_gate)))
        grad_up = low(grad_act * silu_gate)
        grad_norm = low(contract_cols(grad_gate, gate_w) + contract_cols(grad_up, up_w))
        norm_terms[step] = group_reduce(grad_norm.reshape(2, 2, rows, width))
        ffn_part = low(jnp.dot(activation, down_w, preferred_element_type=jnp.float32))
        out_terms[step] = group_reduce(ffn_part.reshape(2, 2, rows, width))
        kept.append((normed, activation, grad_gate, grad_up))
    grad_norm_two = ring_reduce(norm_terms)
    block_out = low(hidden + ring_reduce(out_terms))
    output = order_pair(block_out, over_x(block_out), tensor_at).reshape(1, block_rows, width)

    normed_all, activation_all, grad_gate_all, grad_up_all = (
        jnp.concatenate([parts[i] for parts in kept]) for i in range(4)
    )
    cotangent_all = jnp.concatenate(cotangents)

    def spread_columns(term):
        term = term.reshape(2, 2, 4, width // 16, units)
        term = low(wide(pick(term, y_at)) + wide(over_y(pick(term, 1 - y_at))))
        term = order_pair(pick(term, core_at), over_core(pick(term, 1 - core_at)), core_at)
        term = jnp.moveaxis(term, 0, 2).reshape(4, width // 16, 2 * units)
        return wide(jnp.concatenate(fsdp_spread(term, fsdp_at), axis=1))

    term_gate = low(contract_rows(normed_all, grad_gate_all))
    term_up = low(contract_rows(normed_all, grad_up_all))
    term_down = low(contract_rows(activation_all, cotangent_all))
    grad_w_gate = spread_columns(term_gate)
    grad_w_up = spread_columns(term_up)
    term_down = term_down.reshape(2, unit_half, width)
    term_down = low(wide(pick(term_down, y_at)) + wide(over_y(pick(term_down, 1 - y_at))))
    grad_w_down = wide(
        lax.ppermute(
            term_down,
            ("context", "fsdp"),
            [(c * 4 + f, f * 4 + (c % 2) * 2 + c // 2) for c in range(4) for f in range(4)],
        )
    )

    grad_ffn_gain = gain_reduce(jnp.sum(grad_norm_two * normal_two, axis=0), context_at, fsdp_at)
    grad_hidden = wide(own_cotangent[0]) + norm_backward(
        grad_norm_two, gain_two, inverse_two, normal_two
    )
    hidden_low = plane_gather(low(grad_hidden)).reshape(length, width)
    term_out = low(contract_rows(attended, hidden_low)).reshape(4, head_cols // 4, width)
    grad_w_out = ring_reduce([pick(term_out, (fsdp_at - r) % 4) for r in range(4)])
    grad_attended = low(contract_cols(hidden_low, out_w)).reshape(length, group_size, HEAD)
    grad_query, grad_key, grad_value = attention_backward(
        queries, keys, values, grad_attended, logsum, allowed, score_scale
    )
    grad_turned = jnp.concatenate([grad_query, grad_key[:, None]], axis=1)
    grad_heads = low(unrotate(grad_turned, cos_table, sine_table)).reshape(length, head_cols + kv_cols)
    grad_heads = jnp.concatenate([grad_heads, low(grad_value)], axis=1)
    grad_norm_one = contract_cols(grad_heads, attn_w)
    grad_attn_gain = gain_reduce(jnp.sum(grad_norm_one * normal_one, axis=0), context_at, fsdp_at)
    grad_norm_one = plane_reduce(low(grad_norm_one).reshape(2, 2, 2, rows, width))
    term_heads = low(contract_rows(normed_one, grad_heads))
    term_heads = term_heads.reshape(4, 4, width // 16, head_cols + 2 * kv_cols)
    term_heads = low(ring_reduce([pick(term_heads, (fsdp_at - r) % 4, 1) for r in range(4)]))
    blocks = [wide(block) for block in context_spread(term_heads, context_at)]
    grad_w_query = jnp.concatenate([block[:, :head_cols] for block in blocks], axis=1)
    grad_w_key = jnp.concatenate(
        [block[:, head_cols : head_cols + kv_cols] for block in blocks], axis=1
    )
    grad_w_value = jnp.concatenate([block[:, head_cols + kv_cols :] for block in blocks], axis=1)
    grad_input = low(
        grad_hidden
        + norm_backward(grad_norm_one, gain_one, inverse_one[:rows], normal_one[:rows])
    )
    grad_tokens = order_pair(grad_input, over_x(grad_input), tensor_at)
    return (
        output,
        grad_tokens.reshape(1, block_rows, width),
        grad_attn_gain,
        grad_w_query,
        grad_w_key,
        grad_w_value,
        grad_w_out,
        grad_ffn_gain,
        grad_w_gate,
        grad_w_up,
        grad_w_down,
    )


def solution(mesh):
    sizes = tuple(mesh.shape[a] for a in ("tensor", "context", "fsdp"))
    return jax.shard_map(
        per_device_moved if sizes == (2, 4, 4) else per_device_general,
        mesh=mesh,
        in_specs=(
            P("fsdp", "context", None),
            P("fsdp", None),
            P("fsdp", "context"),
            P("fsdp"),
            P("fsdp", "tensor"),
            P("fsdp", "tensor"),
            P("fsdp", "tensor"),
            P(("tensor", "fsdp"), None),
            P("fsdp"),
            P("fsdp", "tensor"),
            P("fsdp", "tensor"),
            P(("tensor", "fsdp"), None),
            P("fsdp", "context", None),
        ),
        out_specs=(
            P("fsdp", "context", None),
            P("fsdp", "context", None),
            P(("context", "fsdp")),
            P(("context", "fsdp"), "tensor"),
            P(("context", "fsdp"), "tensor"),
            P(("context", "fsdp"), "tensor"),
            P(("tensor", "context", "fsdp"), None),
            P(("context", "fsdp")),
            P(("context", "fsdp"), "tensor"),
            P(("context", "fsdp"), "tensor"),
            P(("tensor", "context", "fsdp"), None),
        ),
        check_vma=False,
    )
```

```python
import functools
import math

import jax
import jax.numpy as jnp
from jax import lax
from jax.experimental import pallas as pl
from jax.experimental.pallas import tpu as pltpu
from jax.sharding import PartitionSpec as P

HEAD = 128
PARTS = 2
NO_COST = pl.CostEstimate(flops=1, bytes_accessed=1, transcendentals=0)


norm_epsilon = 1e-05
rope_base = 1000000.0


def rotary(positions):
    freq_index = jnp.arange(HEAD // 2, dtype=jnp.float32)
    inverse = rope_base ** (-2.0 * freq_index / HEAD)
    angles = positions.astype(jnp.float32)[:, None] * inverse[None, :]
    angles = jnp.concatenate([angles, angles], axis=1)
    return (jnp.cos(angles), jnp.sin(angles))


def rotate(values, cos_table, sine_table):
    half_size = values.shape[-1] // 2
    lower_half = values[..., :half_size]
    upper_half = values[..., half_size:]
    turned = jnp.concatenate([-upper_half, lower_half], axis=-1)
    return values * cos_table[:, None, :] + turned * sine_table[:, None, :]


def unrotate(grad_rot, cos_table, sine_table):
    half_size = grad_rot.shape[-1] // 2
    scaled = grad_rot * sine_table[:, None, :]
    swapped = jnp.concatenate([scaled[..., half_size:], -scaled[..., :half_size]], axis=-1)
    return grad_rot * cos_table[:, None, :] + swapped


def norm_forward(values):
    inverse_rms = lax.rsqrt(jnp.mean(values * values, axis=-1, keepdims=True) + norm_epsilon)
    return (inverse_rms, values * inverse_rms)


def norm_backward(grad_normed, gain, inverse_rms, normalized):
    scaled = grad_normed * gain
    return inverse_rms * (
        scaled - normalized * jnp.mean(scaled * normalized, axis=-1, keepdims=True)
    )


def contract_rows(left, right):
    return lax.dot_general(
        left, right, (((0,), (0,)), ((), ())), preferred_element_type=jnp.float32
    )


def contract_cols(left, right):
    return lax.dot_general(
        left, right, (((1,), (1,)), ((), ())), preferred_element_type=jnp.float32
    )


def block_scores(query_blk, key_all, query_seg, key_seg, query_order, key_order, score_scale):
    scores = (
        jnp.einsum("qhgd,khd->hgqk", query_blk, key_all, preferred_element_type=jnp.float32)
        * score_scale
    )
    allowed = (query_seg[:, None] == key_seg[None, :]) & (
        query_order[:, None] >= key_order[None, :]
    )
    return jnp.where(allowed[None, None], scores, -1e30)


def attend_forward(
    queries, key_all, value_all, query_seg, key_seg, query_order, key_order, block_rows, score_scale
):
    block_count = queries.shape[0] // block_rows

    def one_block(pieces):
        query_blk, seg_blk, order_blk = pieces
        scores = block_scores(
            query_blk, key_all, seg_blk, key_seg, order_blk, key_order, score_scale
        )
        highest = jnp.max(scores, axis=-1, keepdims=True)
        weights = jnp.exp(scores - highest)
        row_total = jnp.sum(weights, axis=-1, keepdims=True)
        probabilities = weights / row_total
        attended = jnp.einsum(
            "hgqk,khd->qhgd",
            probabilities.astype(jnp.bfloat16),
            value_all,
            preferred_element_type=jnp.float32,
        )
        return (attended, highest + jnp.log(row_total))

    stacked = (
        queries.reshape((block_count, block_rows) + queries.shape[1:]),
        query_seg.reshape(block_count, block_rows),
        query_order.reshape(block_count, block_rows),
    )
    attended, logsum = lax.map(one_block, stacked)
    return (attended.reshape(queries.shape), logsum)


def attend_backward(
    queries,
    key_all,
    value_all,
    grad_attended,
    logsum,
    query_seg,
    key_seg,
    query_order,
    key_order,
    block_rows,
    score_scale,
):
    block_count = queries.shape[0] // block_rows
    empty_grad = jnp.zeros(key_all.shape, jnp.float32)

    def one_block(carry, pieces):
        grad_key, grad_value = carry
        query_blk, grad_blk, logsum_blk, seg_blk, order_blk = pieces
        scores = block_scores(
            query_blk, key_all, seg_blk, key_seg, order_blk, key_order, score_scale
        )
        probabilities = jnp.exp(scores - logsum_blk)
        grad_probs = jnp.einsum(
            "qhgd,khd->hgqk", grad_blk, value_all, preferred_element_type=jnp.float32
        )
        row_delta = jnp.sum(probabilities * grad_probs, axis=-1, keepdims=True)
        grad_scores = (probabilities * (grad_probs - row_delta)).astype(jnp.bfloat16)
        grad_query = score_scale * jnp.einsum(
            "hgqk,khd->qhgd", grad_scores, key_all, preferred_element_type=jnp.float32
        )
        grad_key = grad_key + score_scale * jnp.einsum(
            "hgqk,qhgd->khd", grad_scores, query_blk, preferred_element_type=jnp.float32
        )
        grad_value = grad_value + jnp.einsum(
            "hgqk,qhgd->khd",
            probabilities.astype(jnp.bfloat16),
            grad_blk,
            preferred_element_type=jnp.float32,
        )
        return ((grad_key, grad_value), grad_query)

    stacked = (
        queries.reshape((block_count, block_rows) + queries.shape[1:]),
        grad_attended.reshape((block_count, block_rows) + grad_attended.shape[1:]),
        logsum,
        query_seg.reshape(block_count, block_rows),
        query_order.reshape(block_count, block_rows),
    )
    (grad_key, grad_value), grad_query = lax.scan(one_block, (empty_grad, empty_grad), stacked)
    return (grad_query.reshape(queries.shape), grad_key, grad_value)


def per_device_general(
    tokens,
    segments,
    positions,
    attn_gain,
    w_query,
    w_key,
    w_value,
    w_out,
    ffn_gain,
    w_gate,
    w_up,
    w_down,
    cotangent,
):
    token_count = tokens.shape[1]
    residual = tokens[0].astype(jnp.float32)
    seq_start = lax.axis_index("context") * token_count
    key_seg = segments[0]
    key_order = jnp.arange(key_seg.shape[0], dtype=jnp.int32)
    query_seg = lax.dynamic_slice_in_dim(key_seg, seq_start, token_count)
    query_order = seq_start + jnp.arange(token_count, dtype=jnp.int32)
    cos_table, sine_table = rotary(positions[0])
    block_rows = math.gcd(token_count, 512)
    score_scale = 1.0 / math.sqrt(HEAD)
    gain_one, query_w, key_w, value_w, out_w = (
        lax.all_gather(attn_gain, "fsdp", axis=0, tiled=True),
        lax.all_gather(w_query, "fsdp", axis=0, tiled=True),
        lax.all_gather(w_key, "fsdp", axis=0, tiled=True),
        lax.all_gather(w_value, "fsdp", axis=0, tiled=True),
        lax.all_gather(w_out, "fsdp", axis=0, tiled=True),
    )
    gain_two, gate_w, up_w, down_w = (
        lax.all_gather(ffn_gain, "fsdp", axis=0, tiled=True),
        lax.all_gather(w_gate, "fsdp", axis=0, tiled=True),
        lax.all_gather(w_up, "fsdp", axis=0, tiled=True),
        lax.all_gather(w_down, "fsdp", axis=0, tiled=True),
    )
    query_heads = query_w.shape[1] // HEAD
    kv_heads = key_w.shape[1] // HEAD
    group_size = query_heads // kv_heads
    inverse_one, normal_one = norm_forward(residual)
    normed_one = (normal_one * gain_one.astype(jnp.float32)).astype(jnp.bfloat16)
    query_raw = jnp.dot(normed_one, query_w, preferred_element_type=jnp.float32)
    key_raw = jnp.dot(normed_one, key_w, preferred_element_type=jnp.float32)
    value_raw = jnp.dot(normed_one, value_w, preferred_element_type=jnp.float32)
    queries = rotate(
        query_raw.reshape(token_count, query_heads, HEAD), cos_table, sine_table
    ).astype(jnp.bfloat16)
    queries = queries.reshape(token_count, kv_heads, group_size, HEAD)
    key_local = rotate(key_raw.reshape(token_count, kv_heads, HEAD), cos_table, sine_table).astype(
        jnp.bfloat16
    )
    value_local = value_raw.astype(jnp.bfloat16).reshape(token_count, kv_heads, HEAD)
    key_all, value_all = (
        lax.all_gather(key_local, "context", axis=0, tiled=True),
        lax.all_gather(value_local, "context", axis=0, tiled=True),
    )
    attended, logsum = attend_forward(
        queries,
        key_all,
        value_all,
        query_seg,
        key_seg,
        query_order,
        key_order,
        block_rows,
        score_scale,
    )
    attended_low = attended.reshape(token_count, query_heads * HEAD).astype(jnp.bfloat16)
    attn_part = jnp.dot(attended_low, out_w, preferred_element_type=jnp.float32)
    hidden = residual + lax.psum(attn_part, "tensor")
    inverse_two, normal_two = norm_forward(hidden)
    normed_two = (normal_two * gain_two.astype(jnp.float32)).astype(jnp.bfloat16)
    gate_proj = jnp.dot(normed_two, gate_w, preferred_element_type=jnp.float32)
    up_proj = jnp.dot(normed_two, up_w, preferred_element_type=jnp.float32)
    sigmoid_gate = jax.nn.sigmoid(gate_proj)
    silu_gate = gate_proj * sigmoid_gate
    activation = (silu_gate * up_proj).astype(jnp.bfloat16)
    ffn_part = jnp.dot(activation, down_w, preferred_element_type=jnp.float32)
    block_out = hidden + lax.psum(ffn_part.astype(jnp.bfloat16), "tensor").astype(jnp.float32)
    output = block_out.astype(jnp.bfloat16)[None]
    grad_rows = cotangent[0]
    term_down = contract_rows(activation, grad_rows)
    grad_act = contract_cols(grad_rows, down_w)
    grad_gate = (
        grad_act * up_proj * sigmoid_gate * (1.0 + gate_proj * (1.0 - sigmoid_gate))
    ).astype(jnp.bfloat16)
    grad_up = (grad_act * silu_gate).astype(jnp.bfloat16)
    term_gate = contract_rows(normed_two, grad_gate)
    term_up = contract_rows(normed_two, grad_up)
    grad_norm_two = contract_cols(grad_gate, gate_w) + contract_cols(grad_up, up_w)
    grad_norm_two = lax.psum(grad_norm_two, "tensor")
    term_gain_two = jnp.sum(grad_norm_two * normal_two, axis=0)
    grad_hidden = grad_rows.astype(jnp.float32) + norm_backward(
        grad_norm_two, gain_two.astype(jnp.float32), inverse_two, normal_two
    )
    hidden_low = grad_hidden.astype(jnp.bfloat16)
    term_out = contract_rows(attended_low, hidden_low)
    grad_attended = (
        contract_cols(hidden_low, out_w)
        .astype(jnp.bfloat16)
        .reshape(token_count, kv_heads, group_size, HEAD)
    )
    key_back, value_back = (key_all, value_all)
    grad_query, grad_key_all, grad_value_all = attend_backward(
        queries,
        key_back,
        value_back,
        grad_attended,
        logsum,
        query_seg,
        key_seg,
        query_order,
        key_order,
        block_rows,
        score_scale,
    )
    grad_key_rot, grad_value_rot = (
        lax.psum_scatter(grad_key_all, "context", scatter_dimension=0, tiled=True),
        lax.psum_scatter(grad_value_all, "context", scatter_dimension=0, tiled=True),
    )
    grad_query_low = unrotate(
        grad_query.reshape(token_count, query_heads, HEAD), cos_table, sine_table
    )
    grad_query_low = grad_query_low.reshape(token_count, query_heads * HEAD).astype(jnp.bfloat16)
    grad_key_low = (
        unrotate(grad_key_rot, cos_table, sine_table)
        .reshape(token_count, kv_heads * HEAD)
        .astype(jnp.bfloat16)
    )
    grad_value_low = grad_value_rot.reshape(token_count, kv_heads * HEAD).astype(jnp.bfloat16)
    term_query = contract_rows(normed_one, grad_query_low)
    term_key = contract_rows(normed_one, grad_key_low)
    term_value = contract_rows(normed_one, grad_value_low)
    grad_norm_one = (
        contract_cols(grad_query_low, query_w)
        + contract_cols(grad_key_low, key_w)
        + contract_cols(grad_value_low, value_w)
    )
    grad_norm_one = lax.psum(grad_norm_one, "tensor")
    term_gain_one = jnp.sum(grad_norm_one * normal_one, axis=0)
    grad_input = grad_hidden + norm_backward(
        grad_norm_one, gain_one.astype(jnp.float32), inverse_one, normal_one
    )
    summed = (
        lax.psum_scatter(term_gain_one, ("context", "fsdp"), scatter_dimension=0, tiled=True),
        lax.psum_scatter(term_query, ("context", "fsdp"), scatter_dimension=0, tiled=True),
        lax.psum_scatter(term_key, ("context", "fsdp"), scatter_dimension=0, tiled=True),
        lax.psum_scatter(term_value, ("context", "fsdp"), scatter_dimension=0, tiled=True),
        lax.psum_scatter(term_out, ("context", "fsdp"), scatter_dimension=0, tiled=True),
        lax.psum_scatter(term_gain_two, ("context", "fsdp"), scatter_dimension=0, tiled=True),
        lax.psum_scatter(term_gate, ("context", "fsdp"), scatter_dimension=0, tiled=True),
        lax.psum_scatter(term_up, ("context", "fsdp"), scatter_dimension=0, tiled=True),
        lax.psum_scatter(term_down, ("context", "fsdp"), scatter_dimension=0, tiled=True),
    )
    return (
        output,
        grad_input.astype(jnp.bfloat16)[None],
        summed[0],
        summed[1],
        summed[2],
        summed[3],
        summed[4],
        summed[5],
        summed[6],
        summed[7],
        summed[8],
    )


def low(values):
    return values.astype(jnp.bfloat16)


def wide(values):
    return values.astype(jnp.float32)


def matmul(left, right):
    return jnp.dot(left, right, preferred_element_type=jnp.float32)


def fence(*arrays):
    return lax.optimization_barrier(arrays)


def place_pair(mine, theirs, index, axis):
    first = index == 0
    return jnp.concatenate(
        [jnp.where(first, mine, theirs), jnp.where(first, theirs, mine)], axis=axis
    )


def cut(block, index, size, axis):
    return lax.dynamic_slice_in_dim(block, index * size, size, axis=axis)


def over_core(block):
    return lax.ppermute(block, "context", [(i, i ^ 1) for i in range(4)])


def over_y(block):
    return lax.ppermute(block, "context", [(i, i ^ 2) for i in range(4)])


def over_diagonal(block):
    return lax.ppermute(block, "context", [(i, i ^ 3) for i in range(4)])


def over_x(block):
    return lax.ppermute(block, "tensor", [(0, 1), (1, 0)])


def shift_z(block, step=1):
    return lax.ppermute(block, "fsdp", [(i, (i + step) % 4) for i in range(4)])


def exchange_z(block, distance):
    return lax.ppermute(block, "fsdp", [(i, i ^ distance) for i in range(4)])


def gather_z(block):
    return lax.all_gather(block, "fsdp", axis=0, tiled=True)


def scatter_z(block):
    return lax.psum_scatter(block, "fsdp", scatter_dimension=0, tiled=True)


def gain_start(term):
    return term, over_x(term)


def gain_next(term, got, index, exchange, axis=0):
    term = term + got
    kept = lax.dynamic_index_in_dim(term, index, axis, keepdims=False)
    return kept, exchange(lax.dynamic_index_in_dim(term, 1 - index, axis, keepdims=False))


def flat(pieces):
    return [block for piece in pieces for block in piece]


def context_send(blocks, context_at):
    size = blocks.shape[0] // 4
    return (
        cut(blocks, context_at, size, 0),
        over_core(cut(blocks, context_at ^ 1, size, 0)),
        over_y(cut(blocks, context_at ^ 2, size, 0)),
        over_diagonal(cut(blocks, context_at ^ 3, size, 0)),
    )


def context_order(got, context_at):
    got = jnp.stack(got)
    return [lax.dynamic_index_in_dim(got, i ^ context_at, 0, keepdims=False) for i in range(4)]


def dot_dims(left, right, left_dim, right_dim):
    return lax.dot_general(
        left, right, (((left_dim,), (right_dim,)), ((), ())), preferred_element_type=jnp.float32
    )


def attend_kernel(
    scale, block, raw_ref, cos_ref, sine_ref, tag_ref, tag_row_ref, turned_ref, out_ref, sum_ref
):
    length = raw_ref.shape[0]
    heads = out_ref.shape[1] // HEAD

    def turn(rows, cols):
        part = raw_ref[rows, cols]
        return low(part * cos_ref[rows, :] + pltpu.roll(part, HEAD // 2, 1) * sine_ref[rows, :])

    everything = slice(0, length)
    key_cols = slice(heads * HEAD, (heads + 1) * HEAD)
    value_cols = slice((heads + 1) * HEAD, (heads + 2) * HEAD)
    keys = turn(everything, key_cols)
    values = low(raw_ref[:, value_cols])
    turned_ref[:, key_cols] = keys
    turned_ref[:, value_cols] = values
    for start in range(0, length, block):
        rows = slice(start, start + block)
        allowed = (tag_ref[rows, 0:1] == tag_row_ref[0:1, :]) & (
            tag_ref[rows, 1:2] >= tag_row_ref[1:2, :]
        )
        for head in range(heads):
            cols = slice(head * HEAD, (head + 1) * HEAD)
            queries = turn(rows, cols)
            turned_ref[rows, cols] = queries
            scores = jnp.where(allowed, dot_dims(queries, keys, 1, 1) * scale, -1e30)
            highest = jnp.max(scores, axis=-1, keepdims=True)
            weights = jnp.exp(scores - highest)
            row_total = jnp.sum(weights, axis=-1, keepdims=True)
            probabilities = low(weights * (1.0 / row_total))
            out_ref[rows, cols] = low(dot_dims(probabilities, values, 1, 0))
            sum_ref[rows, head : head + 1] = highest + jnp.log(row_total)


def attend_back_kernel(
    scale,
    block,
    turned_ref,
    grad_ref,
    sum_ref,
    cos_ref,
    sine_ref,
    tag_ref,
    tag_row_ref,
    out_ref,
    key_acc,
    value_acc,
):
    length = turned_ref.shape[0]
    heads = grad_ref.shape[1] // HEAD

    def turn_back(part, rows):
        return low(part * cos_ref[rows, :] - pltpu.roll(part, HEAD // 2, 1) * sine_ref[rows, :])

    key_cols = slice(heads * HEAD, (heads + 1) * HEAD)
    value_cols = slice((heads + 1) * HEAD, (heads + 2) * HEAD)
    keys, values = turned_ref[:, key_cols], turned_ref[:, value_cols]
    key_acc[...] = jnp.zeros_like(key_acc)
    value_acc[...] = jnp.zeros_like(value_acc)
    for start in range(0, length, block):
        rows = slice(start, start + block)
        allowed = (tag_ref[rows, 0:1] == tag_row_ref[0:1, :]) & (
            tag_ref[rows, 1:2] >= tag_row_ref[1:2, :]
        )
        for head in range(heads):
            cols = slice(head * HEAD, (head + 1) * HEAD)
            queries, grad = turned_ref[rows, cols], grad_ref[rows, cols]
            scores = jnp.where(allowed, dot_dims(queries, keys, 1, 1) * scale, -1e30)
            probabilities = jnp.exp(scores - sum_ref[rows, head : head + 1])
            grad_probs = dot_dims(grad, values, 1, 1)
            row_delta = jnp.sum(probabilities * grad_probs, axis=-1, keepdims=True)
            grad_scores = low(probabilities * (grad_probs - row_delta))
            out_ref[rows, cols] = turn_back(scale * dot_dims(grad_scores, keys, 1, 0), rows)
            key_acc[...] += dot_dims(grad_scores, queries, 0, 0)
            value_acc[...] += dot_dims(low(probabilities), grad, 0, 0)
    out_ref[:, key_cols] = turn_back(scale * key_acc[...], slice(0, length))
    out_ref[:, value_cols] = low(value_acc[...])


def feed_forward_kernel(*refs):
    tokens_refs, cotangent_refs, (gate_ref, up_ref, down_ref) = refs[:2], refs[2:4], refs[4:7]
    activation_ref, gate_grad_ref, up_grad_ref = refs[7:10]
    norm_refs, part_refs = refs[10:12], refs[12:14]
    size = tokens_refs[0].shape[0]
    for i in range(2):
        rows = slice(i * size, (i + 1) * size)
        gate_proj = dot_dims(tokens_refs[i][...], gate_ref[...], 1, 0)
        up_proj = dot_dims(tokens_refs[i][...], up_ref[...], 1, 0)
        sigmoid_gate = jax.nn.sigmoid(gate_proj)
        silu_gate = gate_proj * sigmoid_gate
        activation = low(silu_gate * up_proj)
        activation_ref[rows, :] = activation
        part_refs[i][...] = low(dot_dims(activation, down_ref[...], 1, 0))
        grad_act = dot_dims(cotangent_refs[i][...], down_ref[...], 1, 1)
        grad_gate = low(
            grad_act * up_proj * sigmoid_gate * (1.0 + gate_proj * (1.0 - sigmoid_gate))
        )
        grad_up = low(grad_act * silu_gate)
        gate_grad_ref[rows, :] = grad_gate
        up_grad_ref[rows, :] = grad_up
        norm_refs[i][...] = low(
            dot_dims(grad_gate, gate_ref[...], 1, 1) + dot_dims(grad_up, up_ref[...], 1, 1)
        )


def feed_forward_local(tokens, cotangents, gate_w, up_w, down_w):
    size, width = tokens[0].shape
    units = gate_w.shape[1]
    small = jax.ShapeDtypeStruct((2 * size, units), jnp.bfloat16)
    large = jax.ShapeDtypeStruct((size, width), jnp.bfloat16)
    return pl.pallas_call(
        feed_forward_kernel,
        out_shape=[small] * 3 + [large] * 4,
        compiler_params=pltpu.CompilerParams(vmem_limit_bytes=48 * 2**20),
        cost_estimate=NO_COST,
    )(*tokens, *cotangents, gate_w, up_w, down_w)


def weight_kernel(count, *refs):
    wide_refs, narrow_refs, (out_ref, acc_ref) = refs[:count], refs[count:-2], refs[-2:]
    size = wide_refs[0].shape[0]
    each = count // len(narrow_refs)
    transposed = out_ref.shape[1] == wide_refs[0].shape[1]
    for i in range(count):
        first = (i % each) * size
        narrow = narrow_refs[i // each][first : first + size, :]
        pair = (narrow, wide_refs[i][...]) if transposed else (wide_refs[i][...], narrow)
        term = dot_dims(*pair, 0, 0)
        if i == 0:
            acc_ref[...] = term
        else:
            acc_ref[...] += term
    out_ref[...] = low(acc_ref[...])


def weight_local(wides, narrows, transposed):
    size, width = wides[0].shape
    length, units = narrows[0].shape
    cols = width // 2
    tile = (units, cols) if transposed else (cols, units)
    return pl.pallas_call(
        functools.partial(weight_kernel, len(wides)),
        grid=(2,),
        in_specs=[pl.BlockSpec((size, cols), lambda i: (0, i))] * len(wides)
        + [pl.BlockSpec((length, units), lambda i: (0, 0))] * len(narrows),
        out_specs=pl.BlockSpec(tile, (lambda i: (0, i)) if transposed else (lambda i: (i, 0))),
        out_shape=jax.ShapeDtypeStruct(
            (units, width) if transposed else (width, units), jnp.bfloat16
        ),
        scratch_shapes=[pltpu.VMEM(tile, jnp.float32)],
        compiler_params=pltpu.CompilerParams(vmem_limit_bytes=48 * 2**20),
        cost_estimate=NO_COST,
    )(*wides, *narrows)


def attend_tables(places, seg, order):
    cos_table, sine_table = rotary(places)
    signs = jnp.where(jnp.arange(HEAD) < HEAD // 2, -1.0, 1.0)
    return cos_table, sine_table * signs, jnp.stack([seg, order], axis=1), jnp.stack([seg, order])


def attend_forward_local(raw, tables, heads, score_scale):
    length = raw.shape[0]
    return pl.pallas_call(
        functools.partial(attend_kernel, score_scale, math.gcd(length, 512)),
        out_shape=[
            jax.ShapeDtypeStruct(raw.shape, jnp.bfloat16),
            jax.ShapeDtypeStruct((length, heads * HEAD), jnp.bfloat16),
            jax.ShapeDtypeStruct((length, heads), jnp.float32),
        ],
        compiler_params=pltpu.CompilerParams(vmem_limit_bytes=48 * 2**20),
        cost_estimate=NO_COST,
    )(raw, *tables)


def attend_backward_local(turned, grad_attended, logsum, tables, heads, score_scale):
    length = turned.shape[0]
    return pl.pallas_call(
        functools.partial(attend_back_kernel, score_scale, math.gcd(length, 512)),
        out_shape=jax.ShapeDtypeStruct(turned.shape, jnp.bfloat16),
        scratch_shapes=[pltpu.VMEM((length, HEAD), jnp.float32)] * 2,
        compiler_params=pltpu.CompilerParams(vmem_limit_bytes=48 * 2**20),
        cost_estimate=NO_COST,
    )(turned, grad_attended, logsum, *tables)


def per_device_moved(
    tokens,
    segments,
    positions,
    attn_gain,
    w_query,
    w_key,
    w_value,
    w_out,
    ffn_gain,
    w_gate,
    w_up,
    w_down,
    cotangent,
):
    tensor_at, context_at, fsdp_at = (lax.axis_index(a) for a in ("tensor", "context", "fsdp"))
    y_at, core_at = context_at // 2, context_at % 2
    places = [(fsdp_at - r) % 4 for r in range(4)]
    width = tokens.shape[2]
    block_rows = tokens.shape[1]
    rows = block_rows // 2
    length = segments.shape[1]
    score_scale = 1.0 / math.sqrt(HEAD)
    shard = attn_gain.shape[0]
    head_cols = w_query.shape[1] // 4
    kv_cols = w_key.shape[1] // 4
    heads = head_cols // HEAD
    all_cols = head_cols + 2 * kv_cols
    unit_half = w_gate.shape[1] // 16
    units = 2 * unit_half

    half_width = width // 2

    def split_x(block):
        first, second = block[:rows], block[rows:]
        return jnp.concatenate(
            [
                jnp.where(tensor_at == 0, first, second),
                jnp.where(tensor_at == 0, second, first),
            ]
        )

    def spread_context(block):
        pair = jnp.concatenate([block, over_y(block)])
        return jnp.concatenate([pair, over_core(pair)])

    own_cotangent = split_x(cotangent[0])
    part = rows // PARTS
    gains = jnp.concatenate([attn_gain, ffn_gain]).reshape(-1, all_cols)
    gain_rows = gains.shape[0] // 2
    pieces = [
        jnp.concatenate(
            [
                cut(w_query, context_at, head_cols, 1),
                cut(w_key, context_at, kv_cols, 1),
                cut(w_value, context_at, kv_cols, 1),
            ],
            axis=1,
        ),
        cut(w_out, context_at, all_cols, 1),
        jnp.pad(gains, ((0, 16 - gains.shape[0]), (0, 0))),
    ]
    packed = lax.all_gather(jnp.concatenate(pieces), "fsdp", axis=0, tiled=False)
    own_tokens = split_x(tokens[0])
    all_tokens = spread_context(own_tokens)
    all_places = spread_context(split_x(positions[0]))

    def unit_weights(place):
        first = ((place * 2 + core_at) * 2 + y_at) * unit_half
        return jnp.concatenate(
            [
                lax.dynamic_slice_in_dim(w_gate, first, unit_half, axis=1),
                lax.dynamic_slice_in_dim(w_up, first, unit_half, axis=1),
            ],
            axis=1,
        )

    unit_own = unit_weights(fsdp_at)
    unit_out = [unit_weights((fsdp_at + step) % 4) for step in (1, 2, 3)]
    down_w = cut(w_down, core_at, units, 0)

    def flip(block, axis, index):
        return jnp.where(index == 0, block, jnp.flip(block, axis))

    def relative(block):
        block = block.reshape(2, 2, 2, rows)
        block = flip(flip(flip(block, 0, y_at), 1, core_at), 2, tensor_at)
        return jnp.swapaxes(block, 0, 1).reshape(length)

    order = relative(jnp.arange(length, dtype=jnp.int32))
    tables = attend_tables(all_places, relative(segments[0]), order)
    residual = wide(all_tokens)
    inverse_one = lax.rsqrt(jnp.mean(residual * residual, axis=-1, keepdims=True) + norm_epsilon)
    all_tokens, unit_own = fence(all_tokens, unit_own)
    packed, unit_own_given, all_tokens, inverse_one, own_cotangent, *rest = fence(
        packed, over_y(unit_own), all_tokens, inverse_one, own_cotangent, *unit_out, *tables
    )
    unit_out, tables = rest[:3], rest[3:]

    at = [0]
    for piece in pieces:
        at.append(at[-1] + piece.shape[0])
    attn_w = packed[:, : at[1]].reshape(width, all_cols)
    out_part = packed[:, at[1] : at[2]].reshape(4 * w_out.shape[0], all_cols)
    gain_one = wide(packed[:, at[2] : at[2] + gain_rows].reshape(width))
    gain_two = wide(packed[:, at[2] + gain_rows : at[2] + 2 * gain_rows].reshape(width))
    cot_own = [gather_z(own_cotangent[:part]), None]
    unit_got = [shift_z(unit_out[0], 1), unit_out[1], shift_z(unit_out[2], 3)]
    out_got = context_send(out_part, context_at)
    normed_one = low(wide(all_tokens) * inverse_one * gain_one)
    turned, attended, logsum = attend_forward_local(
        matmul(normed_one, attn_w), tables, heads, score_scale
    )
    attended, cot_own[0], cot_late, *rest = fence(
        attended, cot_own[0], own_cotangent[part:rows], *unit_got, *out_got
    )
    unit_got, out_got = rest[:3], rest[3:]

    unit_got[1] = shift_z(unit_got[1], 2)
    cot_own[1] = gather_z(cot_late)
    cot_x = [over_x(cot_own[0])]
    out_w = jnp.concatenate(context_order(out_got, context_at), axis=1)
    part_shape = (2, 2, rows, width)

    def plane_first(theirs, mine):
        return low(wide(mine) + wide(over_core(theirs)))

    def plane_second(mine):
        left, right = mine[..., :half_width], mine[..., half_width:]
        return left[:, 0], over_x(left[:, 1]), right[0], over_y(right[1])

    def plane_third(left, left_got, right, right_got):
        left = low(wide(left) + wide(left_got))
        right = low(wide(right) + wide(right_got))
        return left[0], over_y(left[1]), right[0], over_x(right[1])

    def plane_last(left, left_got, right, right_got):
        return jnp.concatenate(
            [wide(left) + wide(left_got), wide(right) + wide(right_got)], axis=-1
        )

    theirs = low(matmul(attended[length // 2 :], out_w)).reshape(part_shape)
    mine = low(matmul(attended[: length // 2], out_w)).reshape(part_shape)
    (mine,) = fence(plane_first(theirs, mine))
    parts = fence(*plane_second(mine))
    parts = fence(*plane_third(*parts), unit_got[1], cot_x[0], cot_own[1])
    unit_got[1], cot_x[0], cot_own[1] = parts[4:]
    own_residual = wide(own_tokens[:rows])
    hidden = own_residual + plane_last(*parts[:4])
    inverse_two, normal_two = norm_forward(hidden)
    normed_two = low(normal_two * gain_two)
    normed_two, cot_own[1], cot_own[0], cot_x[0], unit_got[0], unit_got[1], unit_got[2] = fence(
        normed_two, cot_own[1], cot_own[0], cot_x[0], *unit_got
    )

    normed_own = [gather_z(normed_two[:part])]
    unit_given = [over_y(jnp.concatenate([unit_got[0], unit_got[2]]))]
    cot_x.append(over_x(cot_own[1]))
    cot_core = [[over_core(cot_own[0]), over_core(cot_x[0])]]
    own_units = jnp.zeros((width, units), jnp.bfloat16)
    other_units = lax.dynamic_update_slice_in_dim(own_units, unit_own_given, places[0] * shard, 0)
    for r, block in enumerate([unit_own] + list(unit_got)):
        own_units = lax.dynamic_update_slice_in_dim(own_units, block, places[r] * shard, 0)
    (
        normed_own[0],
        cot_x[1],
        later,
        cot_own[1],
        own_units,
        other_units,
        unit_given[0],
        unit_got[1],
        *cot_core[0],
    ) = fence(
        normed_own[0],
        cot_x[1],
        normed_two[part:],
        cot_own[1],
        own_units,
        other_units,
        unit_given[0],
        unit_got[1],
        *cot_core[0],
    )

    normed_own.append(gather_z(later))
    normed_x = [over_x(normed_own[0])]
    unit_given.append(over_y(unit_got[1]))
    cot_core.append([over_core(cot_own[1]), over_core(cot_x[1])])
    for block, place in (
        (unit_given[0][:shard], places[1]),
        (unit_given[0][shard:], places[3]),
        (unit_given[1], places[2]),
    ):
        other_units = lax.dynamic_update_slice_in_dim(other_units, block, place * shard, 0)
    normed_core = over_core(normed_own[0])
    (
        normed_own[1],
        normed_x[0],
        normed_core,
        own_units,
        other_units,
        cot_own[1],
        cot_x[1],
        *cot_core[1],
    ) = fence(
        normed_own[1],
        normed_x[0],
        normed_core,
        own_units,
        other_units,
        cot_own[1],
        cot_x[1],
        *cot_core[1],
    )
    gate_w = place_pair(own_units[:, :unit_half], other_units[:, :unit_half], y_at, 1)
    up_w = place_pair(own_units[:, unit_half:], other_units[:, unit_half:], y_at, 1)

    def total(mine, theirs):
        return low(wide(mine) + wide(theirs))

    def piece_of(i, k, normed):
        cot = ((cot_own, cot_x)[k][i], cot_core[i][k])
        small = feed_forward_local(normed, cot, gate_w, up_w, down_w)
        return list(normed) + list(cot) + list(small)

    def send_y(term):
        return over_y(cut(term, 1 - y_at, half_width, 0))

    gate_w, up_w, normed_x[0], normed_own[1], normed_x_core = fence(
        gate_w, up_w, normed_x[0], normed_own[1], over_core(normed_x[0])
    )
    kept = [None] * 4
    normed_x.append(over_x(normed_own[1]))
    kept[1] = piece_of(0, 1, (normed_x[0], normed_x_core))
    kept[0] = piece_of(0, 0, (normed_own[0], normed_core))
    normed_x[1], normed_own[1], *rest = fence(normed_x[1], normed_own[1], *kept[1], *kept[0])
    kept[1], kept[0] = rest[:11], rest[11:]
    give_core, keep_core, normed_x_core, normed_late, *rest = fence(
        over_core(kept[1][8]),
        over_core(kept[0][8]),
        over_core(normed_x[1]),
        over_core(normed_own[1]),
        normed_x[1],
        normed_own[1],
        kept[1][7],
        kept[0][7],
    )
    normed_x[1], normed_own[1], give, keep = rest
    keeps = [total(keep, keep_core)]
    give_x = [over_x(total(give, give_core))]
    kept[3] = piece_of(1, 1, (normed_x[1], normed_x_core))
    give_x[0], keeps[0], normed_late, normed_own[1], *kept[3] = fence(
        give_x[0], keeps[0], normed_late, normed_own[1], *kept[3]
    )
    give_core, norm_term, give, normed_late, normed_own[1] = fence(
        over_core(kept[3][8]), total(keeps[0], give_x[0]), kept[3][7], normed_late, normed_own[1]
    )

    norm_two = [scatter_z(norm_term)]
    give_x.append(over_x(total(give, give_core)))
    kept[2] = piece_of(1, 0, (normed_own[1], normed_late))

    def weight_sum(wide_at, narrow_at, transposed=False):
        return weight_local(
            flat(piece[wide_at : wide_at + 2] for piece in kept),
            [piece[narrow_at] for piece in kept],
            transposed,
        )

    term_gate = weight_sum(0, 5)
    give_x[1], norm_two[0], term_gate, *rest = fence(
        give_x[1], norm_two[0], term_gate, *flat(kept)
    )
    kept = [rest[11 * i : 11 * i + 11] for i in range(4)]
    keep_core, keep, give_x[1], term_gate, out_keep, out_keep_core, out_give, out_give_core, *rest = fence(
        over_core(kept[2][8]),
        kept[2][7],
        give_x[1],
        term_gate,
        kept[0][9],
        over_core(kept[0][10]),
        kept[1][9],
        over_core(kept[1][10]),
        *flat(kept),
    )
    kept = [rest[11 * i : 11 * i + 11] for i in range(4)]

    def unit_sum(term, given):
        term = low(wide(cut(term, y_at, half_width, 0)) + wide(given))
        return cut(term, core_at, half_width // 2, 0), over_core(
            cut(term, 1 - core_at, half_width // 2, 0)
        )

    def to_owners(term):
        return [cut(term, fsdp_at, width // 16, 0)] + [
            shift_z(cut(term, (fsdp_at + step) % 4, width // 16, 0), step) for step in (1, 2, 3)
        ]

    norm_two.append(scatter_z(low(wide(keep) + wide(keep_core) + wide(give_x[1]))))
    gate_given = send_y(term_gate)
    out_x = [over_x(total(out_give, out_give_core))]
    out_first = total(out_keep, out_keep_core)
    term_up = weight_sum(0, 6)
    term_down = weight_sum(2, 4, True)
    norm_two[1], gate_given, out_x[0], term_up, term_down, *rest = fence(
        norm_two[1],
        gate_given,
        out_x[0],
        term_up,
        term_down,
        out_first,
        *kept[2][9:],
        *kept[3][9:],
    )
    out_first, parts_late = rest[0], [rest[1:3], rest[3:5]]

    grad_norm_two = wide(jnp.concatenate(norm_two))
    grad_hidden = wide(own_cotangent[:rows]) + norm_backward(
        grad_norm_two, gain_two, inverse_two, normal_two
    )
    hidden_low = low(grad_hidden)
    left, right = hidden_low[:, :half_width], hidden_low[:, half_width:]
    gate_pair = unit_sum(term_gate, gate_given)
    gain_two_sum = gain_start(jnp.sum(grad_norm_two * normal_two, axis=0).reshape(2, 2, 2, 2, -1))
    left, left_got, right, right_got, *rest = fence(
        left, over_x(left), right, over_y(right), *gate_pair, *gain_two_sum
    )
    gate_pair, gain_two_sum = rest[:2], rest[2:]
    gain_two_sum = gain_next(*gain_two_sum, core_at, over_core, 1)
    gate_term = place_pair(*gate_pair, core_at, 1)
    ffn_out = [scatter_z(low(wide(out_first) + wide(out_x[0])))]
    left = jnp.stack([left, left_got])
    right = jnp.stack([right, right_got])
    left, left_got, right, right_got, gate_term, *gain_two_sum = fence(
        left, over_y(left), right, over_x(right), gate_term, *gain_two_sum
    )
    gain_two_sum = gain_next(*gain_two_sum, y_at, over_y)
    mine = jnp.concatenate(
        [jnp.stack([left, left_got]), jnp.stack([right, right_got], axis=1)], axis=-1
    )
    mine, theirs, gate_term, ffn_out[0], *gain_two_sum = fence(
        mine, over_core(mine), gate_term, ffn_out[0], *gain_two_sum
    )

    hidden_low = jnp.stack([mine, theirs]).reshape(length, width)
    gate_sent = to_owners(gate_term)
    grad_attended = low(contract_cols(hidden_low, out_w))
    grad_heads = attend_backward_local(turned, grad_attended, logsum, tables, heads, score_scale)
    grad_heads, hidden_low, *rest = fence(grad_heads, hidden_low, *gate_sent, *gain_two_sum)
    gate_sent, gain_two_sum = rest[:4], rest[4:]

    high, lowest = fsdp_at // 2, fsdp_at % 2
    gain_two_sum = gain_next(*gain_two_sum, high, functools.partial(exchange_z, distance=2))
    theirs = low(contract_cols(grad_heads[length // 2 :], attn_w)).reshape(part_shape)
    theirs = over_core(theirs)
    mine = low(contract_cols(grad_heads[: length // 2], attn_w)).reshape(part_shape)
    term_heads = contract_rows(normed_one, grad_heads)
    gain_term = jnp.sum(term_heads * wide(attn_w), axis=1) / gain_one
    term_heads = low(term_heads).reshape(4, 4, width // 16, all_cols).swapaxes(0, 1)
    mine, theirs, term_heads, gain_term, *gain_two_sum = fence(
        mine, theirs, term_heads.reshape(width, all_cols), gain_term, *gain_two_sum
    )
    owned_heads = scatter_z(term_heads)
    gain_one_sum = gain_start(gain_term.reshape(2, 2, 2, 2, -1))
    gain_two_sum = gain_next(*gain_two_sum, lowest, functools.partial(exchange_z, distance=1))
    parts = fence(*plane_second(total(mine, theirs)), *gain_one_sum, *gain_two_sum, *flat(parts_late))
    gain_one_sum = gain_next(*parts[4:6], core_at, over_core, 1)
    grad_ffn_gain = parts[6] + parts[7]
    parts_late = [parts[8:10], parts[10:12]]
    out_last = [(first, over_core(second)) for first, second in parts_late]
    parts = fence(*plane_third(*parts[:4]), *flat(out_last), *gain_one_sum, term_up, term_down)
    grad_norm_one = plane_last(*parts[:4])
    out_last = [total(*parts[4:6]), total(*parts[6:8])]
    gain_one_sum = gain_next(*parts[8:10], y_at, over_y)
    term_up, term_down = parts[10:]
    normal_one = own_residual * inverse_one[:rows]
    grad_input = low(
        grad_hidden + norm_backward(grad_norm_one, gain_one, inverse_one[:rows], normal_one)
    )

    up_given = send_y(term_up)
    out_x.append(over_x(out_last[1]))
    out_x[1], up_given, grad_input, term_down, hidden_low, owned_heads, *gain_one_sum = fence(
        out_x[1], up_given, grad_input, term_down, hidden_low, owned_heads, *gain_one_sum
    )

    ffn_out.append(scatter_z(low(wide(out_last[0]) + wide(out_x[1]))))
    down_cols = [cut(term_down, i, half_width, 1) for i in (y_at, 1 - y_at)]
    down_given = over_y(down_cols[1])
    grad_tokens = place_pair(grad_input, over_x(grad_input), tensor_at, 0)
    up_pair = unit_sum(term_up, up_given)
    up_sent = to_owners(place_pair(*up_pair, core_at, 1))
    heads_got = context_send(owned_heads, context_at)
    gain_one_sum = gain_next(*gain_one_sum, high, functools.partial(exchange_z, distance=2))
    gain_one_sum = gain_next(*gain_one_sum, lowest, functools.partial(exchange_z, distance=1))
    grad_attn_gain = gain_one_sum[0] + gain_one_sum[1]
    grad_w_out = wide(scatter_z(low(contract_rows(attended, hidden_low))))
    down_sum = low(wide(down_cols[0]) + wide(down_given))
    quarter = half_width // 2
    down_blocks = place_pair(
        cut(down_sum, core_at, quarter, 1),
        over_core(cut(down_sum, 1 - core_at, quarter, 1)),
        core_at,
        0,
    )
    down_got = [cut(down_blocks, fsdp_at, unit_half, 0)] + [
        shift_z(cut(down_blocks, (fsdp_at + step) % 4, unit_half, 0), step) for step in (1, 2, 3)
    ]
    block_out = low(hidden + wide(jnp.concatenate(ffn_out)))
    output = place_pair(block_out, over_x(block_out), tensor_at, 0)
    got = context_order(heads_got, context_at)
    grad_w_query = wide(jnp.concatenate([block[:, :head_cols] for block in got], axis=1))
    grad_w_key = wide(
        jnp.concatenate([block[:, head_cols : head_cols + kv_cols] for block in got], axis=1)
    )
    grad_w_value = wide(jnp.concatenate([block[:, head_cols + kv_cols :] for block in got], axis=1))
    unit_owned = []
    for got in (gate_sent, up_sent):
        owned = jnp.zeros((width // 16, 8 * units), jnp.float32)
        for r in range(4):
            owned = lax.dynamic_update_slice_in_dim(owned, wide(got[r]), places[r] * 2 * units, 1)
        unit_owned.append(owned)
    grad_w_gate, grad_w_up = unit_owned
    down_stack = jnp.stack(down_got)
    down_blocks = jnp.concatenate(
        [
            lax.dynamic_index_in_dim(down_stack, (fsdp_at - i) % 4, 0, keepdims=False)
            for i in range(4)
        ]
    )
    got = context_order(context_send(down_blocks, context_at), context_at)
    grad_w_down = wide(jnp.concatenate(got, axis=1))
    return (
        output[None],
        grad_tokens[None],
        grad_attn_gain,
        grad_w_query,
        grad_w_key,
        grad_w_value,
        grad_w_out,
        grad_ffn_gain,
        grad_w_gate,
        grad_w_up,
        grad_w_down,
    )


def solution(mesh):
    sizes = tuple(mesh.shape[a] for a in ("tensor", "context", "fsdp"))
    return jax.shard_map(
        per_device_moved if sizes == (2, 4, 4) else per_device_general,
        mesh=mesh,
        in_specs=(
            P("fsdp", "context", None),
            P("fsdp", None),
            P("fsdp", "context"),
            P("fsdp"),
            P("fsdp", "tensor"),
            P("fsdp", "tensor"),
            P("fsdp", "tensor"),
            P(("tensor", "fsdp"), None),
            P("fsdp"),
            P("fsdp", "tensor"),
            P("fsdp", "tensor"),
            P(("tensor", "fsdp"), None),
            P("fsdp", "context", None),
        ),
        out_specs=(
            P("fsdp", "context", None),
            P("fsdp", "context", None),
            P(("context", "fsdp")),
            P(("context", "fsdp"), "tensor"),
            P(("context", "fsdp"), "tensor"),
            P(("context", "fsdp"), "tensor"),
            P(("tensor", "context", "fsdp"), None),
            P(("context", "fsdp")),
            P(("context", "fsdp"), "tensor"),
            P(("context", "fsdp"), "tensor"),
            P(("tensor", "context", "fsdp"), None),
        ),
        check_vma=False,
    )
```

```python
import functools
import math

import jax
import jax.numpy as jnp
from jax import lax
from jax.experimental import pallas as pl
from jax.experimental.pallas import tpu as pltpu
from jax.sharding import PartitionSpec as P

HEAD = 128
PARTS = 2
NO_COST = pl.CostEstimate(flops=1, bytes_accessed=1, transcendentals=0)


norm_epsilon = 1e-05
rope_base = 1000000.0


def rotary(positions):
    freq_index = jnp.arange(HEAD // 2, dtype=jnp.float32)
    inverse = rope_base ** (-2.0 * freq_index / HEAD)
    angles = positions.astype(jnp.float32)[:, None] * inverse[None, :]
    angles = jnp.concatenate([angles, angles], axis=1)
    return (jnp.cos(angles), jnp.sin(angles))


def rotate(values, cos_table, sine_table):
    half_size = values.shape[-1] // 2
    lower_half = values[..., :half_size]
    upper_half = values[..., half_size:]
    turned = jnp.concatenate([-upper_half, lower_half], axis=-1)
    return values * cos_table[:, None, :] + turned * sine_table[:, None, :]


def unrotate(grad_rot, cos_table, sine_table):
    half_size = grad_rot.shape[-1] // 2
    scaled = grad_rot * sine_table[:, None, :]
    swapped = jnp.concatenate([scaled[..., half_size:], -scaled[..., :half_size]], axis=-1)
    return grad_rot * cos_table[:, None, :] + swapped


def norm_forward(values):
    inverse_rms = lax.rsqrt(jnp.mean(values * values, axis=-1, keepdims=True) + norm_epsilon)
    return (inverse_rms, values * inverse_rms)


def norm_backward(grad_normed, gain, inverse_rms, normalized):
    scaled = grad_normed * gain
    return inverse_rms * (
        scaled - normalized * jnp.mean(scaled * normalized, axis=-1, keepdims=True)
    )


def contract_rows(left, right):
    return lax.dot_general(
        left, right, (((0,), (0,)), ((), ())), preferred_element_type=jnp.float32
    )


def contract_cols(left, right):
    return lax.dot_general(
        left, right, (((1,), (1,)), ((), ())), preferred_element_type=jnp.float32
    )


def block_scores(query_blk, key_all, query_seg, key_seg, query_order, key_order, score_scale):
    scores = (
        jnp.einsum("qhgd,khd->hgqk", query_blk, key_all, preferred_element_type=jnp.float32)
        * score_scale
    )
    allowed = (query_seg[:, None] == key_seg[None, :]) & (
        query_order[:, None] >= key_order[None, :]
    )
    return jnp.where(allowed[None, None], scores, -1e30)


def attend_forward(
    queries, key_all, value_all, query_seg, key_seg, query_order, key_order, block_rows, score_scale
):
    block_count = queries.shape[0] // block_rows

    def one_block(pieces):
        query_blk, seg_blk, order_blk = pieces
        scores = block_scores(
            query_blk, key_all, seg_blk, key_seg, order_blk, key_order, score_scale
        )
        highest = jnp.max(scores, axis=-1, keepdims=True)
        weights = jnp.exp(scores - highest)
        row_total = jnp.sum(weights, axis=-1, keepdims=True)
        probabilities = weights / row_total
        attended = jnp.einsum(
            "hgqk,khd->qhgd",
            probabilities.astype(jnp.bfloat16),
            value_all,
            preferred_element_type=jnp.float32,
        )
        return (attended, highest + jnp.log(row_total))

    stacked = (
        queries.reshape((block_count, block_rows) + queries.shape[1:]),
        query_seg.reshape(block_count, block_rows),
        query_order.reshape(block_count, block_rows),
    )
    attended, logsum = lax.map(one_block, stacked)
    return (attended.reshape(queries.shape), logsum)


def attend_backward(
    queries,
    key_all,
    value_all,
    grad_attended,
    logsum,
    query_seg,
    key_seg,
    query_order,
    key_order,
    block_rows,
    score_scale,
):
    block_count = queries.shape[0] // block_rows
    empty_grad = jnp.zeros(key_all.shape, jnp.float32)

    def one_block(carry, pieces):
        grad_key, grad_value = carry
        query_blk, grad_blk, logsum_blk, seg_blk, order_blk = pieces
        scores = block_scores(
            query_blk, key_all, seg_blk, key_seg, order_blk, key_order, score_scale
        )
        probabilities = jnp.exp(scores - logsum_blk)
        grad_probs = jnp.einsum(
            "qhgd,khd->hgqk", grad_blk, value_all, preferred_element_type=jnp.float32
        )
        row_delta = jnp.sum(probabilities * grad_probs, axis=-1, keepdims=True)
        grad_scores = (probabilities * (grad_probs - row_delta)).astype(jnp.bfloat16)
        grad_query = score_scale * jnp.einsum(
            "hgqk,khd->qhgd", grad_scores, key_all, preferred_element_type=jnp.float32
        )
        grad_key = grad_key + score_scale * jnp.einsum(
            "hgqk,qhgd->khd", grad_scores, query_blk, preferred_element_type=jnp.float32
        )
        grad_value = grad_value + jnp.einsum(
            "hgqk,qhgd->khd",
            probabilities.astype(jnp.bfloat16),
            grad_blk,
            preferred_element_type=jnp.float32,
        )
        return ((grad_key, grad_value), grad_query)

    stacked = (
        queries.reshape((block_count, block_rows) + queries.shape[1:]),
        grad_attended.reshape((block_count, block_rows) + grad_attended.shape[1:]),
        logsum,
        query_seg.reshape(block_count, block_rows),
        query_order.reshape(block_count, block_rows),
    )
    (grad_key, grad_value), grad_query = lax.scan(one_block, (empty_grad, empty_grad), stacked)
    return (grad_query.reshape(queries.shape), grad_key, grad_value)


def per_device_general(
    tokens,
    segments,
    positions,
    attn_gain,
    w_query,
    w_key,
    w_value,
    w_out,
    ffn_gain,
    w_gate,
    w_up,
    w_down,
    cotangent,
):
    token_count = tokens.shape[1]
    residual = tokens[0].astype(jnp.float32)
    seq_start = lax.axis_index("context") * token_count
    key_seg = segments[0]
    key_order = jnp.arange(key_seg.shape[0], dtype=jnp.int32)
    query_seg = lax.dynamic_slice_in_dim(key_seg, seq_start, token_count)
    query_order = seq_start + jnp.arange(token_count, dtype=jnp.int32)
    cos_table, sine_table = rotary(positions[0])
    block_rows = math.gcd(token_count, 512)
    score_scale = 1.0 / math.sqrt(HEAD)
    gain_one, query_w, key_w, value_w, out_w = (
        lax.all_gather(attn_gain, "fsdp", axis=0, tiled=True),
        lax.all_gather(w_query, "fsdp", axis=0, tiled=True),
        lax.all_gather(w_key, "fsdp", axis=0, tiled=True),
        lax.all_gather(w_value, "fsdp", axis=0, tiled=True),
        lax.all_gather(w_out, "fsdp", axis=0, tiled=True),
    )
    gain_two, gate_w, up_w, down_w = (
        lax.all_gather(ffn_gain, "fsdp", axis=0, tiled=True),
        lax.all_gather(w_gate, "fsdp", axis=0, tiled=True),
        lax.all_gather(w_up, "fsdp", axis=0, tiled=True),
        lax.all_gather(w_down, "fsdp", axis=0, tiled=True),
    )
    query_heads = query_w.shape[1] // HEAD
    kv_heads = key_w.shape[1] // HEAD
    group_size = query_heads // kv_heads
    inverse_one, normal_one = norm_forward(residual)
    normed_one = (normal_one * gain_one.astype(jnp.float32)).astype(jnp.bfloat16)
    query_raw = jnp.dot(normed_one, query_w, preferred_element_type=jnp.float32)
    key_raw = jnp.dot(normed_one, key_w, preferred_element_type=jnp.float32)
    value_raw = jnp.dot(normed_one, value_w, preferred_element_type=jnp.float32)
    queries = rotate(
        query_raw.reshape(token_count, query_heads, HEAD), cos_table, sine_table
    ).astype(jnp.bfloat16)
    queries = queries.reshape(token_count, kv_heads, group_size, HEAD)
    key_local = rotate(key_raw.reshape(token_count, kv_heads, HEAD), cos_table, sine_table).astype(
        jnp.bfloat16
    )
    value_local = value_raw.astype(jnp.bfloat16).reshape(token_count, kv_heads, HEAD)
    key_all, value_all = (
        lax.all_gather(key_local, "context", axis=0, tiled=True),
        lax.all_gather(value_local, "context", axis=0, tiled=True),
    )
    attended, logsum = attend_forward(
        queries,
        key_all,
        value_all,
        query_seg,
        key_seg,
        query_order,
        key_order,
        block_rows,
        score_scale,
    )
    attended_low = attended.reshape(token_count, query_heads * HEAD).astype(jnp.bfloat16)
    attn_part = jnp.dot(attended_low, out_w, preferred_element_type=jnp.float32)
    hidden = residual + lax.psum(attn_part, "tensor")
    inverse_two, normal_two = norm_forward(hidden)
    normed_two = (normal_two * gain_two.astype(jnp.float32)).astype(jnp.bfloat16)
    gate_proj = jnp.dot(normed_two, gate_w, preferred_element_type=jnp.float32)
    up_proj = jnp.dot(normed_two, up_w, preferred_element_type=jnp.float32)
    sigmoid_gate = jax.nn.sigmoid(gate_proj)
    silu_gate = gate_proj * sigmoid_gate
    activation = (silu_gate * up_proj).astype(jnp.bfloat16)
    ffn_part = jnp.dot(activation, down_w, preferred_element_type=jnp.float32)
    block_out = hidden + lax.psum(ffn_part.astype(jnp.bfloat16), "tensor").astype(jnp.float32)
    output = block_out.astype(jnp.bfloat16)[None]
    grad_rows = cotangent[0]
    term_down = contract_rows(activation, grad_rows)
    grad_act = contract_cols(grad_rows, down_w)
    grad_gate = (
        grad_act * up_proj * sigmoid_gate * (1.0 + gate_proj * (1.0 - sigmoid_gate))
    ).astype(jnp.bfloat16)
    grad_up = (grad_act * silu_gate).astype(jnp.bfloat16)
    term_gate = contract_rows(normed_two, grad_gate)
    term_up = contract_rows(normed_two, grad_up)
    grad_norm_two = contract_cols(grad_gate, gate_w) + contract_cols(grad_up, up_w)
    grad_norm_two = lax.psum(grad_norm_two, "tensor")
    term_gain_two = jnp.sum(grad_norm_two * normal_two, axis=0)
    grad_hidden = grad_rows.astype(jnp.float32) + norm_backward(
        grad_norm_two, gain_two.astype(jnp.float32), inverse_two, normal_two
    )
    hidden_low = grad_hidden.astype(jnp.bfloat16)
    term_out = contract_rows(attended_low, hidden_low)
    grad_attended = (
        contract_cols(hidden_low, out_w)
        .astype(jnp.bfloat16)
        .reshape(token_count, kv_heads, group_size, HEAD)
    )
    key_back, value_back = (key_all, value_all)
    grad_query, grad_key_all, grad_value_all = attend_backward(
        queries,
        key_back,
        value_back,
        grad_attended,
        logsum,
        query_seg,
        key_seg,
        query_order,
        key_order,
        block_rows,
        score_scale,
    )
    grad_key_rot, grad_value_rot = (
        lax.psum_scatter(grad_key_all, "context", scatter_dimension=0, tiled=True),
        lax.psum_scatter(grad_value_all, "context", scatter_dimension=0, tiled=True),
    )
    grad_query_low = unrotate(
        grad_query.reshape(token_count, query_heads, HEAD), cos_table, sine_table
    )
    grad_query_low = grad_query_low.reshape(token_count, query_heads * HEAD).astype(jnp.bfloat16)
    grad_key_low = (
        unrotate(grad_key_rot, cos_table, sine_table)
        .reshape(token_count, kv_heads * HEAD)
        .astype(jnp.bfloat16)
    )
    grad_value_low = grad_value_rot.reshape(token_count, kv_heads * HEAD).astype(jnp.bfloat16)
    term_query = contract_rows(normed_one, grad_query_low)
    term_key = contract_rows(normed_one, grad_key_low)
    term_value = contract_rows(normed_one, grad_value_low)
    grad_norm_one = (
        contract_cols(grad_query_low, query_w)
        + contract_cols(grad_key_low, key_w)
        + contract_cols(grad_value_low, value_w)
    )
    grad_norm_one = lax.psum(grad_norm_one, "tensor")
    term_gain_one = jnp.sum(grad_norm_one * normal_one, axis=0)
    grad_input = grad_hidden + norm_backward(
        grad_norm_one, gain_one.astype(jnp.float32), inverse_one, normal_one
    )
    summed = (
        lax.psum_scatter(term_gain_one, ("context", "fsdp"), scatter_dimension=0, tiled=True),
        lax.psum_scatter(term_query, ("context", "fsdp"), scatter_dimension=0, tiled=True),
        lax.psum_scatter(term_key, ("context", "fsdp"), scatter_dimension=0, tiled=True),
        lax.psum_scatter(term_value, ("context", "fsdp"), scatter_dimension=0, tiled=True),
        lax.psum_scatter(term_out, ("context", "fsdp"), scatter_dimension=0, tiled=True),
        lax.psum_scatter(term_gain_two, ("context", "fsdp"), scatter_dimension=0, tiled=True),
        lax.psum_scatter(term_gate, ("context", "fsdp"), scatter_dimension=0, tiled=True),
        lax.psum_scatter(term_up, ("context", "fsdp"), scatter_dimension=0, tiled=True),
        lax.psum_scatter(term_down, ("context", "fsdp"), scatter_dimension=0, tiled=True),
    )
    return (
        output,
        grad_input.astype(jnp.bfloat16)[None],
        summed[0],
        summed[1],
        summed[2],
        summed[3],
        summed[4],
        summed[5],
        summed[6],
        summed[7],
        summed[8],
    )


def low(values):
    return values.astype(jnp.bfloat16)


def wide(values):
    return values.astype(jnp.float32)


def matmul(left, right):
    return jnp.dot(left, right, preferred_element_type=jnp.float32)


def fence(*arrays):
    return lax.optimization_barrier(arrays)


def place_pair(mine, theirs, index, axis):
    first = index == 0
    return jnp.concatenate(
        [jnp.where(first, mine, theirs), jnp.where(first, theirs, mine)], axis=axis
    )


def cut(block, index, size, axis):
    return lax.dynamic_slice_in_dim(block, index * size, size, axis=axis)


def over_core(block):
    return lax.ppermute(block, "context", [(i, i ^ 1) for i in range(4)])


def over_y(block):
    return lax.ppermute(block, "context", [(i, i ^ 2) for i in range(4)])


def over_diagonal(block):
    return lax.ppermute(block, "context", [(i, i ^ 3) for i in range(4)])


def over_x(block):
    return lax.ppermute(block, "tensor", [(0, 1), (1, 0)])


def shift_z(block, step=1):
    return lax.ppermute(block, "fsdp", [(i, (i + step) % 4) for i in range(4)])


def gather_z(block):
    return lax.all_gather(block, "fsdp", axis=0, tiled=True)


def scatter_z(block):
    return lax.psum_scatter(block, "fsdp", scatter_dimension=0, tiled=True)


def gain_start(term):
    return term, over_x(term)


def gain_next(term, got, index, exchange, axis=0):
    term = term + got
    kept = lax.dynamic_index_in_dim(term, index, axis, keepdims=False)
    return kept, exchange(lax.dynamic_index_in_dim(term, 1 - index, axis, keepdims=False))


def flat(pieces):
    return [block for piece in pieces for block in piece]


def context_send(blocks, context_at):
    size = blocks.shape[0] // 4
    return (
        cut(blocks, context_at, size, 0),
        over_core(cut(blocks, context_at ^ 1, size, 0)),
        over_y(cut(blocks, context_at ^ 2, size, 0)),
        over_diagonal(cut(blocks, context_at ^ 3, size, 0)),
    )


def context_order(got, context_at):
    got = jnp.stack(got)
    return [lax.dynamic_index_in_dim(got, i ^ context_at, 0, keepdims=False) for i in range(4)]


def dot_dims(left, right, left_dim, right_dim):
    return lax.dot_general(
        left, right, (((left_dim,), (right_dim,)), ((), ())), preferred_element_type=jnp.float32
    )


def attend_kernel(
    scale, block, raw_ref, cos_ref, sine_ref, tag_ref, tag_row_ref, turned_ref, out_ref, sum_ref
):
    length = raw_ref.shape[0]
    heads = out_ref.shape[1] // HEAD

    def turn(rows, cols):
        part = raw_ref[rows, cols]
        return low(part * cos_ref[rows, :] + pltpu.roll(part, HEAD // 2, 1) * sine_ref[rows, :])

    everything = slice(0, length)
    key_cols = slice(heads * HEAD, (heads + 1) * HEAD)
    value_cols = slice((heads + 1) * HEAD, (heads + 2) * HEAD)
    keys = turn(everything, key_cols)
    values = low(raw_ref[:, value_cols])
    turned_ref[:, key_cols] = keys
    turned_ref[:, value_cols] = values
    for start in range(0, length, block):
        rows = slice(start, start + block)
        allowed = (tag_ref[rows, 0:1] == tag_row_ref[0:1, :]) & (
            tag_ref[rows, 1:2] >= tag_row_ref[1:2, :]
        )
        for head in range(heads):
            cols = slice(head * HEAD, (head + 1) * HEAD)
            queries = turn(rows, cols)
            turned_ref[rows, cols] = queries
            scores = jnp.where(allowed, dot_dims(queries, keys, 1, 1) * scale, -1e30)
            highest = jnp.max(scores, axis=-1, keepdims=True)
            weights = jnp.exp(scores - highest)
            row_total = jnp.sum(weights, axis=-1, keepdims=True)
            probabilities = low(weights * (1.0 / row_total))
            out_ref[rows, cols] = low(dot_dims(probabilities, values, 1, 0))
            sum_ref[rows, head : head + 1] = highest + jnp.log(row_total)


def attend_back_kernel(
    scale,
    block,
    turned_ref,
    grad_ref,
    sum_ref,
    cos_ref,
    sine_ref,
    tag_ref,
    tag_row_ref,
    out_ref,
    key_acc,
    value_acc,
):
    length = turned_ref.shape[0]
    heads = grad_ref.shape[1] // HEAD

    def turn_back(part, rows):
        return low(part * cos_ref[rows, :] - pltpu.roll(part, HEAD // 2, 1) * sine_ref[rows, :])

    key_cols = slice(heads * HEAD, (heads + 1) * HEAD)
    value_cols = slice((heads + 1) * HEAD, (heads + 2) * HEAD)
    keys, values = turned_ref[:, key_cols], turned_ref[:, value_cols]
    key_acc[...] = jnp.zeros_like(key_acc)
    value_acc[...] = jnp.zeros_like(value_acc)
    for start in range(0, length, block):
        rows = slice(start, start + block)
        allowed = (tag_ref[rows, 0:1] == tag_row_ref[0:1, :]) & (
            tag_ref[rows, 1:2] >= tag_row_ref[1:2, :]
        )
        for head in range(heads):
            cols = slice(head * HEAD, (head + 1) * HEAD)
            queries, grad = turned_ref[rows, cols], grad_ref[rows, cols]
            scores = jnp.where(allowed, dot_dims(queries, keys, 1, 1) * scale, -1e30)
            probabilities = jnp.exp(scores - sum_ref[rows, head : head + 1])
            grad_probs = dot_dims(grad, values, 1, 1)
            row_delta = jnp.sum(probabilities * grad_probs, axis=-1, keepdims=True)
            grad_scores = low(probabilities * (grad_probs - row_delta))
            out_ref[rows, cols] = turn_back(scale * dot_dims(grad_scores, keys, 1, 0), rows)
            key_acc[...] += dot_dims(grad_scores, queries, 0, 0)
            value_acc[...] += dot_dims(low(probabilities), grad, 0, 0)
    out_ref[:, key_cols] = turn_back(scale * key_acc[...], slice(0, length))
    out_ref[:, value_cols] = low(value_acc[...])


def feed_forward_kernel(*refs):
    tokens_refs, cotangent_refs, (gate_ref, up_ref, down_ref) = refs[:2], refs[2:4], refs[4:7]
    activation_ref, gate_grad_ref, up_grad_ref = refs[7:10]
    norm_refs, part_refs = refs[10:12], refs[12:14]
    size = tokens_refs[0].shape[0]
    for i in range(2):
        rows = slice(i * size, (i + 1) * size)
        gate_proj = dot_dims(tokens_refs[i][...], gate_ref[...], 1, 0)
        up_proj = dot_dims(tokens_refs[i][...], up_ref[...], 1, 0)
        sigmoid_gate = jax.nn.sigmoid(gate_proj)
        silu_gate = gate_proj * sigmoid_gate
        activation = low(silu_gate * up_proj)
        activation_ref[rows, :] = activation
        part_refs[i][...] = low(dot_dims(activation, down_ref[...], 1, 0))
        grad_act = dot_dims(cotangent_refs[i][...], down_ref[...], 1, 1)
        grad_gate = low(
            grad_act * up_proj * sigmoid_gate * (1.0 + gate_proj * (1.0 - sigmoid_gate))
        )
        grad_up = low(grad_act * silu_gate)
        gate_grad_ref[rows, :] = grad_gate
        up_grad_ref[rows, :] = grad_up
        norm_refs[i][...] = low(
            dot_dims(grad_gate, gate_ref[...], 1, 1) + dot_dims(grad_up, up_ref[...], 1, 1)
        )


def feed_forward_local(tokens, cotangents, gate_w, up_w, down_w):
    size, width = tokens[0].shape
    units = gate_w.shape[1]
    small = jax.ShapeDtypeStruct((2 * size, units), jnp.bfloat16)
    large = jax.ShapeDtypeStruct((size, width), jnp.bfloat16)
    return pl.pallas_call(
        feed_forward_kernel,
        out_shape=[small] * 3 + [large] * 4,
        compiler_params=pltpu.CompilerParams(vmem_limit_bytes=48 * 2**20),
        cost_estimate=NO_COST,
    )(*tokens, *cotangents, gate_w, up_w, down_w)


def weight_kernel(count, *refs):
    wide_refs, narrow_refs, (out_ref, acc_ref) = refs[:count], refs[count:-2], refs[-2:]
    size = wide_refs[0].shape[0]
    each = count // len(narrow_refs)
    transposed = out_ref.shape[1] == wide_refs[0].shape[1]
    for i in range(count):
        first = (i % each) * size
        narrow = narrow_refs[i // each][first : first + size, :]
        pair = (narrow, wide_refs[i][...]) if transposed else (wide_refs[i][...], narrow)
        term = dot_dims(*pair, 0, 0)
        if i == 0:
            acc_ref[...] = term
        else:
            acc_ref[...] += term
    out_ref[...] = low(acc_ref[...])


def weight_local(wides, narrows, transposed):
    size, width = wides[0].shape
    length, units = narrows[0].shape
    cols = width // 2
    tile = (units, cols) if transposed else (cols, units)
    return pl.pallas_call(
        functools.partial(weight_kernel, len(wides)),
        grid=(2,),
        in_specs=[pl.BlockSpec((size, cols), lambda i: (0, i))] * len(wides)
        + [pl.BlockSpec((length, units), lambda i: (0, 0))] * len(narrows),
        out_specs=pl.BlockSpec(tile, (lambda i: (0, i)) if transposed else (lambda i: (i, 0))),
        out_shape=jax.ShapeDtypeStruct(
            (units, width) if transposed else (width, units), jnp.bfloat16
        ),
        scratch_shapes=[pltpu.VMEM(tile, jnp.float32)],
        compiler_params=pltpu.CompilerParams(vmem_limit_bytes=48 * 2**20),
        cost_estimate=NO_COST,
    )(*wides, *narrows)


def attend_tables(places, seg, order):
    cos_table, sine_table = rotary(places)
    signs = jnp.where(jnp.arange(HEAD) < HEAD // 2, -1.0, 1.0)
    return cos_table, sine_table * signs, jnp.stack([seg, order], axis=1), jnp.stack([seg, order])


def attend_forward_local(raw, tables, heads, score_scale):
    length = raw.shape[0]
    return pl.pallas_call(
        functools.partial(attend_kernel, score_scale, math.gcd(length, 512)),
        out_shape=[
            jax.ShapeDtypeStruct(raw.shape, jnp.bfloat16),
            jax.ShapeDtypeStruct((length, heads * HEAD), jnp.bfloat16),
            jax.ShapeDtypeStruct((length, heads), jnp.float32),
        ],
        compiler_params=pltpu.CompilerParams(vmem_limit_bytes=48 * 2**20),
        cost_estimate=NO_COST,
    )(raw, *tables)


def attend_backward_local(turned, grad_attended, logsum, tables, heads, score_scale):
    length = turned.shape[0]
    return pl.pallas_call(
        functools.partial(attend_back_kernel, score_scale, math.gcd(length, 512)),
        out_shape=jax.ShapeDtypeStruct(turned.shape, jnp.bfloat16),
        scratch_shapes=[pltpu.VMEM((length, HEAD), jnp.float32)] * 2,
        compiler_params=pltpu.CompilerParams(vmem_limit_bytes=48 * 2**20),
        cost_estimate=NO_COST,
    )(turned, grad_attended, logsum, *tables)


def per_device_moved(
    tokens,
    segments,
    positions,
    attn_gain,
    w_query,
    w_key,
    w_value,
    w_out,
    ffn_gain,
    w_gate,
    w_up,
    w_down,
    cotangent,
):
    tensor_at, context_at, fsdp_at = (lax.axis_index(a) for a in ("tensor", "context", "fsdp"))
    y_at, core_at = context_at // 2, context_at % 2
    places = [(fsdp_at - r) % 4 for r in range(4)]
    width = tokens.shape[2]
    block_rows = tokens.shape[1]
    rows = block_rows // 2
    length = segments.shape[1]
    score_scale = 1.0 / math.sqrt(HEAD)
    shard = attn_gain.shape[0]
    head_cols = w_query.shape[1] // 4
    kv_cols = w_key.shape[1] // 4
    heads = head_cols // HEAD
    all_cols = head_cols + 2 * kv_cols
    unit_half = w_gate.shape[1] // 16
    units = 2 * unit_half

    half_width = width // 2

    def split_x(block):
        first, second = block[:rows], block[rows:]
        return jnp.concatenate(
            [
                jnp.where(tensor_at == 0, first, second),
                jnp.where(tensor_at == 0, second, first),
            ]
        )

    def spread_context(block):
        pair = jnp.concatenate([block, over_y(block)])
        return jnp.concatenate([pair, over_core(pair)])

    own_cotangent = split_x(cotangent[0])
    part = rows // PARTS
    gains = jnp.concatenate([attn_gain, ffn_gain]).reshape(-1, all_cols)
    gain_rows = gains.shape[0] // 2
    pieces = [
        jnp.concatenate(
            [
                cut(w_query, context_at, head_cols, 1),
                cut(w_key, context_at, kv_cols, 1),
                cut(w_value, context_at, kv_cols, 1),
            ],
            axis=1,
        ),
        cut(w_out, context_at, all_cols, 1),
        jnp.pad(gains, ((0, 16 - gains.shape[0]), (0, 0))),
    ]
    packed = lax.all_gather(jnp.concatenate(pieces), "fsdp", axis=0, tiled=False)
    own_tokens = split_x(tokens[0])
    all_tokens = spread_context(own_tokens)
    all_places = spread_context(split_x(positions[0]))

    def unit_weights(place):
        first = ((place * 2 + core_at) * 2 + y_at) * unit_half
        return jnp.concatenate(
            [
                lax.dynamic_slice_in_dim(w_gate, first, unit_half, axis=1),
                lax.dynamic_slice_in_dim(w_up, first, unit_half, axis=1),
            ],
            axis=1,
        )

    unit_own = unit_weights(fsdp_at)
    unit_out = [unit_weights((fsdp_at + step) % 4) for step in (1, 2, 3)]
    down_w = cut(w_down, core_at, units, 0)

    def flip(block, axis, index):
        return jnp.where(index == 0, block, jnp.flip(block, axis))

    def relative(block):
        block = block.reshape(2, 2, 2, rows)
        block = flip(flip(flip(block, 0, y_at), 1, core_at), 2, tensor_at)
        return jnp.swapaxes(block, 0, 1).reshape(length)

    order = relative(jnp.arange(length, dtype=jnp.int32))
    tables = attend_tables(all_places, relative(segments[0]), order)
    residual = wide(all_tokens)
    inverse_one = lax.rsqrt(jnp.mean(residual * residual, axis=-1, keepdims=True) + norm_epsilon)
    all_tokens, unit_own = fence(all_tokens, unit_own)
    packed, unit_own_given, all_tokens, inverse_one, own_cotangent, down_w, *rest = fence(
        packed, over_y(unit_own), all_tokens, inverse_one, own_cotangent, down_w, *unit_out, *tables
    )
    unit_out, tables = rest[:3], rest[3:]

    at = [0]
    for piece in pieces:
        at.append(at[-1] + piece.shape[0])
    attn_w = packed[:, : at[1]].reshape(width, all_cols)
    out_part = packed[:, at[1] : at[2]].reshape(4 * w_out.shape[0], all_cols)
    gain_one = wide(packed[:, at[2] : at[2] + gain_rows].reshape(width))
    gain_two = wide(packed[:, at[2] + gain_rows : at[2] + 2 * gain_rows].reshape(width))
    cot_own = [gather_z(own_cotangent[:part]), None]
    unit_got = [shift_z(unit_out[0], 1), unit_out[1], shift_z(unit_out[2], 3)]
    out_got = context_send(out_part, context_at)
    normed_one = low(wide(all_tokens) * inverse_one * gain_one)
    turned, attended, logsum = attend_forward_local(
        matmul(normed_one, attn_w), tables, heads, score_scale
    )
    attended, cot_own[0], cot_late, *rest = fence(
        attended, cot_own[0], own_cotangent[part:rows], *unit_got, *out_got
    )
    unit_got, out_got = rest[:3], rest[3:]

    unit_got[1] = shift_z(unit_got[1], 2)
    cot_own[1] = gather_z(cot_late)
    cot_x = [over_x(cot_own[0])]
    out_w = jnp.concatenate(context_order(out_got, context_at), axis=1)
    part_shape = (2, 2, rows, width)

    def plane_first(theirs, mine):
        return low(wide(mine) + wide(over_core(theirs)))

    def plane_second(mine):
        left, right = mine[..., :half_width], mine[..., half_width:]
        return left[:, 0], over_x(left[:, 1]), right[0], over_y(right[1])

    def plane_third(left, left_got, right, right_got):
        left = low(wide(left) + wide(left_got))
        right = low(wide(right) + wide(right_got))
        return left[0], over_y(left[1]), right[0], over_x(right[1])

    def plane_last(left, left_got, right, right_got):
        return jnp.concatenate(
            [wide(left) + wide(left_got), wide(right) + wide(right_got)], axis=-1
        )

    theirs = low(matmul(attended[length // 2 :], out_w)).reshape(part_shape)
    mine = low(matmul(attended[: length // 2], out_w)).reshape(part_shape)
    (mine,) = fence(plane_first(theirs, mine))
    parts = fence(*plane_second(mine))
    parts = fence(*plane_third(*parts), unit_got[1], cot_x[0], cot_own[1])
    unit_got[1], cot_x[0], cot_own[1] = parts[4:]
    own_residual = wide(own_tokens[:rows])
    hidden = own_residual + plane_last(*parts[:4])
    inverse_two, normal_two = norm_forward(hidden)
    normed_two = low(normal_two * gain_two)
    normed_two, cot_own[1], cot_own[0], cot_x[0], unit_got[0], unit_got[1], unit_got[2] = fence(
        normed_two, cot_own[1], cot_own[0], cot_x[0], *unit_got
    )

    normed_own = [gather_z(normed_two[:part])]
    unit_given = [over_y(jnp.concatenate([unit_got[0], unit_got[2]]))]
    cot_x.append(over_x(cot_own[1]))
    cot_core = [[over_core(cot_own[0]), over_core(cot_x[0])]]
    own_units = jnp.zeros((width, units), jnp.bfloat16)
    other_units = lax.dynamic_update_slice_in_dim(own_units, unit_own_given, places[0] * shard, 0)
    for r, block in enumerate([unit_own] + list(unit_got)):
        own_units = lax.dynamic_update_slice_in_dim(own_units, block, places[r] * shard, 0)
    (
        normed_own[0],
        cot_x[1],
        later,
        cot_own[1],
        own_units,
        other_units,
        unit_given[0],
        unit_got[1],
        *cot_core[0],
    ) = fence(
        normed_own[0],
        cot_x[1],
        normed_two[part:],
        cot_own[1],
        own_units,
        other_units,
        unit_given[0],
        unit_got[1],
        *cot_core[0],
    )

    normed_own.append(gather_z(later))
    normed_x = [over_x(normed_own[0])]
    unit_given.append(over_y(unit_got[1]))
    cot_core.append([over_core(cot_own[1]), over_core(cot_x[1])])
    for block, place in (
        (unit_given[0][:shard], places[1]),
        (unit_given[0][shard:], places[3]),
        (unit_given[1], places[2]),
    ):
        other_units = lax.dynamic_update_slice_in_dim(other_units, block, place * shard, 0)
    normed_core = over_core(normed_own[0])
    (
        normed_own[1],
        normed_x[0],
        normed_core,
        own_units,
        other_units,
        cot_own[1],
        cot_x[1],
        *cot_core[1],
    ) = fence(
        normed_own[1],
        normed_x[0],
        normed_core,
        own_units,
        other_units,
        cot_own[1],
        cot_x[1],
        *cot_core[1],
    )
    gate_w = place_pair(own_units[:, :unit_half], other_units[:, :unit_half], y_at, 1)
    up_w = place_pair(own_units[:, unit_half:], other_units[:, unit_half:], y_at, 1)

    def total(mine, theirs):
        return low(wide(mine) + wide(theirs))

    def piece_of(i, k, normed):
        cot = ((cot_own, cot_x)[k][i], cot_core[i][k])
        small = feed_forward_local(normed, cot, gate_w, up_w, down_w)
        return list(normed) + list(cot) + list(small)

    def send_y(term):
        return over_y(cut(term, 1 - y_at, half_width, 0))

    gate_w, up_w, normed_x[0], normed_own[1], normed_x_core = fence(
        gate_w, up_w, normed_x[0], normed_own[1], over_core(normed_x[0])
    )
    kept = [None] * 4
    normed_x.append(over_x(normed_own[1]))
    kept[1] = piece_of(0, 1, (normed_x[0], normed_x_core))
    kept[0] = piece_of(0, 0, (normed_own[0], normed_core))
    normed_x[1], normed_own[1], *rest = fence(normed_x[1], normed_own[1], *kept[1], *kept[0])
    kept[1], kept[0] = rest[:11], rest[11:]
    give_core, keep_core, normed_x_core, normed_late, *rest = fence(
        over_core(kept[1][8]),
        over_core(kept[0][8]),
        over_core(normed_x[1]),
        over_core(normed_own[1]),
        normed_x[1],
        normed_own[1],
        kept[1][7],
        kept[0][7],
    )
    normed_x[1], normed_own[1], give, keep = rest
    keeps = [total(keep, keep_core)]
    give_x = [over_x(total(give, give_core))]
    kept[3] = piece_of(1, 1, (normed_x[1], normed_x_core))
    give_x[0], keeps[0], normed_late, normed_own[1], *kept[3] = fence(
        give_x[0], keeps[0], normed_late, normed_own[1], *kept[3]
    )
    give_core, norm_term, give, normed_late, normed_own[1] = fence(
        over_core(kept[3][8]), total(keeps[0], give_x[0]), kept[3][7], normed_late, normed_own[1]
    )

    norm_two = [scatter_z(norm_term)]
    give_x.append(over_x(total(give, give_core)))
    kept[2] = piece_of(1, 0, (normed_own[1], normed_late))

    def weight_sum(wide_at, narrow_at, transposed=False):
        return weight_local(
            flat(piece[wide_at : wide_at + 2] for piece in kept),
            [piece[narrow_at] for piece in kept],
            transposed,
        )

    term_gate = weight_sum(0, 5)
    give_x[1], norm_two[0], term_gate, *rest = fence(
        give_x[1], norm_two[0], term_gate, *flat(kept)
    )
    kept = [rest[11 * i : 11 * i + 11] for i in range(4)]
    keep_core, keep, give_x[1], term_gate, out_keep, out_keep_core, out_give, out_give_core, *rest = fence(
        over_core(kept[2][8]),
        kept[2][7],
        give_x[1],
        term_gate,
        kept[0][9],
        over_core(kept[0][10]),
        kept[1][9],
        over_core(kept[1][10]),
        *flat(kept),
    )
    kept = [rest[11 * i : 11 * i + 11] for i in range(4)]

    def unit_sum(term, given):
        term = low(wide(cut(term, y_at, half_width, 0)) + wide(given))
        return cut(term, core_at, half_width // 2, 0), over_core(
            cut(term, 1 - core_at, half_width // 2, 0)
        )

    def to_owners(term):
        return [cut(term, fsdp_at, width // 16, 0)] + [
            shift_z(cut(term, (fsdp_at + step) % 4, width // 16, 0), step) for step in (1, 2, 3)
        ]

    norm_two.append(scatter_z(low(wide(keep) + wide(keep_core) + wide(give_x[1]))))
    gate_given = send_y(term_gate)
    out_x = [over_x(total(out_give, out_give_core))]
    out_first = total(out_keep, out_keep_core)
    term_up = weight_sum(0, 6)
    term_down = weight_sum(2, 4, True)
    norm_two[1], gate_given, out_x[0], term_up, term_down, *rest = fence(
        norm_two[1],
        gate_given,
        out_x[0],
        term_up,
        term_down,
        out_first,
        *kept[2][9:],
        *kept[3][9:],
    )
    out_first, parts_late = rest[0], [rest[1:3], rest[3:5]]

    grad_norm_two = wide(jnp.concatenate(norm_two))
    grad_hidden = wide(own_cotangent[:rows]) + norm_backward(
        grad_norm_two, gain_two, inverse_two, normal_two
    )
    hidden_low = low(grad_hidden)
    left, right = hidden_low[:, :half_width], hidden_low[:, half_width:]
    gate_pair = unit_sum(term_gate, gate_given)
    def gain_send(term):
        term = term.reshape(2, 2, 4, -1)
        parts = [
            lax.dynamic_index_in_dim(term, (fsdp_at + step) % 4, 2, keepdims=False)
            for step in range(4)
        ]
        return parts[:1] + [shift_z(parts[step], step) for step in (1, 2, 3)]

    gain_two_all = gain_send(jnp.sum(grad_norm_two * normal_two, axis=0))
    left, left_got, right, right_got, *rest = fence(
        left, over_x(left), right, over_y(right), *gate_pair, *gain_two_all
    )
    gate_pair, gain_two_sum = rest[:2], gain_start(sum(rest[2:]))
    gate_term = place_pair(*gate_pair, core_at, 1)
    ffn_out = [scatter_z(low(wide(out_first) + wide(out_x[0])))]
    left = jnp.stack([left, left_got])
    right = jnp.stack([right, right_got])
    out_last = flat((first, over_core(second)) for first, second in parts_late)
    left, left_got, right, right_got, gate_term, *rest = fence(
        left, over_y(left), right, over_x(right), gate_term, *gain_two_sum, *out_last
    )
    gain_two_sum, out_last = rest[:2], [total(*rest[2:4]), total(*rest[4:])]
    gain_two_sum = gain_next(*gain_two_sum, core_at, over_core, 1)
    mine = jnp.concatenate(
        [jnp.stack([left, left_got]), jnp.stack([right, right_got], axis=1)], axis=-1
    )
    mine, theirs, gate_term, ffn_out[0], term_up, *rest = fence(
        mine, over_core(mine), gate_term, ffn_out[0], term_up, *gain_two_sum, *out_last
    )
    gain_two_sum, out_last = rest[:2], rest[2:]

    hidden_low = jnp.stack([mine, theirs]).reshape(length, width)
    gate_sent = to_owners(gate_term)
    owned_out = scatter_z(low(contract_rows(attended, hidden_low)))
    up_given = send_y(term_up)
    out_x.append(over_x(out_last[1]))
    grad_attended = low(contract_cols(hidden_low, out_w))
    grad_heads = attend_backward_local(turned, grad_attended, logsum, tables, heads, score_scale)
    gain_two_sum = gain_next(*gain_two_sum, y_at, over_y)
    grad_heads, hidden_low, *gain_two_sum = fence(grad_heads, hidden_low, *gain_two_sum)
    grad_ffn_gain = gain_two_sum[0] + gain_two_sum[1]

    theirs = low(contract_cols(grad_heads[length // 2 :], attn_w)).reshape(part_shape)
    theirs = over_core(theirs)
    mine = low(contract_cols(grad_heads[: length // 2], attn_w)).reshape(part_shape)
    term_heads = contract_rows(normed_one, grad_heads)
    gain_term = jnp.sum(term_heads * wide(attn_w), axis=1) / gain_one
    term_heads = low(term_heads).reshape(4, 4, width // 16, all_cols).swapaxes(0, 1)
    mine, theirs, term_heads, gain_term, owned_out, term_up, up_given, out_x[1], *gate_sent = fence(
        mine,
        theirs,
        term_heads.reshape(width, all_cols),
        gain_term,
        owned_out,
        term_up,
        up_given,
        out_x[1],
        *gate_sent,
    )
    up_pair = unit_sum(term_up, up_given)
    owned_heads = scatter_z(term_heads)
    gain_one_all = gain_send(gain_term)
    parts = fence(*plane_second(total(mine, theirs)), *gain_one_all, *up_pair)
    gain_one_sum = gain_start(sum(parts[4:8]))
    grad_w_out = wide(owned_out)
    up_term = place_pair(*parts[8:], core_at, 1)
    parts = fence(*plane_third(*parts[:4]), *gain_one_sum, up_term, term_down, *out_last)
    grad_norm_one = plane_last(*parts[:4])
    gain_one_sum = gain_next(*parts[4:6], core_at, over_core, 1)
    up_term, term_down = parts[6:8]
    out_last = parts[8:]
    normal_one = own_residual * inverse_one[:rows]
    grad_input = low(
        grad_hidden + norm_backward(grad_norm_one, gain_one, inverse_one[:rows], normal_one)
    )

    out_term = low(wide(out_last[0]) + wide(out_x[1]))
    down_cols = [cut(term_down, i, half_width, 1) for i in (y_at, 1 - y_at)]
    down_given = over_y(down_cols[1])
    grad_input_x = over_x(grad_input)
    down_given, grad_input, grad_input_x, up_term, *gain_one_sum = fence(
        down_given, grad_input, grad_input_x, up_term, *gain_one_sum
    )
    grad_tokens = place_pair(grad_input, grad_input_x, tensor_at, 0)
    down_sum = low(wide(down_cols[0]) + wide(down_given))
    quarter = half_width // 2
    down_own, down_core, up_term, out_term, owned_heads = fence(
        cut(down_sum, core_at, quarter, 1),
        over_core(cut(down_sum, 1 - core_at, quarter, 1)),
        up_term,
        out_term,
        owned_heads,
    )
    ffn_out.append(scatter_z(out_term))

    down_blocks = place_pair(down_own, down_core, core_at, 0)
    down_got = [cut(down_blocks, fsdp_at, unit_half, 0)] + [
        shift_z(cut(down_blocks, (fsdp_at + step) % 4, unit_half, 0), step) for step in (1, 2, 3)
    ]
    heads_got = context_send(owned_heads, context_at)
    gain_one_sum = gain_next(*gain_one_sum, y_at, over_y)
    up_term, ffn_out[1], *rest = fence(
        up_term, ffn_out[1], *down_got, *heads_got, *gain_one_sum
    )
    down_got, heads_got = rest[:4], rest[4:8]
    grad_attn_gain = rest[8] + rest[9]
    up_sent = to_owners(up_term)
    block_out = low(hidden + wide(jnp.concatenate(ffn_out)))
    output = place_pair(block_out, over_x(block_out), tensor_at, 0)
    got = context_order(heads_got, context_at)
    grad_w_query = wide(jnp.concatenate([block[:, :head_cols] for block in got], axis=1))
    grad_w_key = wide(
        jnp.concatenate([block[:, head_cols : head_cols + kv_cols] for block in got], axis=1)
    )
    grad_w_value = wide(jnp.concatenate([block[:, head_cols + kv_cols :] for block in got], axis=1))
    unit_owned = []
    for got in (gate_sent, up_sent):
        owned = jnp.zeros((width // 16, 8 * units), jnp.float32)
        for r in range(4):
            owned = lax.dynamic_update_slice_in_dim(owned, wide(got[r]), places[r] * 2 * units, 1)
        unit_owned.append(owned)
    grad_w_gate, grad_w_up = unit_owned
    down_stack = jnp.stack(down_got)
    down_blocks = jnp.concatenate(
        [
            lax.dynamic_index_in_dim(down_stack, (fsdp_at - i) % 4, 0, keepdims=False)
            for i in range(4)
        ]
    )
    got = context_order(context_send(down_blocks, context_at), context_at)
    grad_w_down = wide(jnp.concatenate(got, axis=1))
    return (
        output[None],
        grad_tokens[None],
        grad_attn_gain,
        grad_w_query,
        grad_w_key,
        grad_w_value,
        grad_w_out,
        grad_ffn_gain,
        grad_w_gate,
        grad_w_up,
        grad_w_down,
    )


def solution(mesh):
    sizes = tuple(mesh.shape[a] for a in ("tensor", "context", "fsdp"))
    return jax.shard_map(
        per_device_moved if sizes == (2, 4, 4) else per_device_general,
        mesh=mesh,
        in_specs=(
            P("fsdp", "context", None),
            P("fsdp", None),
            P("fsdp", "context"),
            P("fsdp"),
            P("fsdp", "tensor"),
            P("fsdp", "tensor"),
            P("fsdp", "tensor"),
            P(("tensor", "fsdp"), None),
            P("fsdp"),
            P("fsdp", "tensor"),
            P("fsdp", "tensor"),
            P(("tensor", "fsdp"), None),
            P("fsdp", "context", None),
        ),
        out_specs=(
            P("fsdp", "context", None),
            P("fsdp", "context", None),
            P(("context", "fsdp")),
            P(("context", "fsdp"), "tensor"),
            P(("context", "fsdp"), "tensor"),
            P(("context", "fsdp"), "tensor"),
            P(("tensor", "context", "fsdp"), None),
            P(("context", "fsdp")),
            P(("context", "fsdp"), "tensor"),
            P(("context", "fsdp"), "tensor"),
            P(("tensor", "context", "fsdp"), None),
        ),
        check_vma=False,
    )
```

```python
import functools
import math

import jax
import jax.numpy as jnp
from jax import lax
from jax.experimental import pallas as pl
from jax.experimental.pallas import tpu as pltpu
from jax.sharding import PartitionSpec as P

HEAD = 128
PARTS = 2
NO_COST = pl.CostEstimate(flops=1, bytes_accessed=1, transcendentals=0)


norm_epsilon = 1e-05
rope_base = 1000000.0


def rotary(positions):
    freq_index = jnp.arange(HEAD // 2, dtype=jnp.float32)
    inverse = rope_base ** (-2.0 * freq_index / HEAD)
    angles = positions.astype(jnp.float32)[:, None] * inverse[None, :]
    angles = jnp.concatenate([angles, angles], axis=1)
    return (jnp.cos(angles), jnp.sin(angles))


def rotate(values, cos_table, sine_table):
    half_size = values.shape[-1] // 2
    lower_half = values[..., :half_size]
    upper_half = values[..., half_size:]
    turned = jnp.concatenate([-upper_half, lower_half], axis=-1)
    return values * cos_table[:, None, :] + turned * sine_table[:, None, :]


def unrotate(grad_rot, cos_table, sine_table):
    half_size = grad_rot.shape[-1] // 2
    scaled = grad_rot * sine_table[:, None, :]
    swapped = jnp.concatenate([scaled[..., half_size:], -scaled[..., :half_size]], axis=-1)
    return grad_rot * cos_table[:, None, :] + swapped


def norm_forward(values):
    inverse_rms = lax.rsqrt(jnp.mean(values * values, axis=-1, keepdims=True) + norm_epsilon)
    return (inverse_rms, values * inverse_rms)


def norm_backward(grad_normed, gain, inverse_rms, normalized):
    scaled = grad_normed * gain
    return inverse_rms * (
        scaled - normalized * jnp.mean(scaled * normalized, axis=-1, keepdims=True)
    )


def contract_rows(left, right):
    return lax.dot_general(
        left, right, (((0,), (0,)), ((), ())), preferred_element_type=jnp.float32
    )


def contract_cols(left, right):
    return lax.dot_general(
        left, right, (((1,), (1,)), ((), ())), preferred_element_type=jnp.float32
    )


def block_scores(query_blk, key_all, query_seg, key_seg, query_order, key_order, score_scale):
    scores = (
        jnp.einsum("qhgd,khd->hgqk", query_blk, key_all, preferred_element_type=jnp.float32)
        * score_scale
    )
    allowed = (query_seg[:, None] == key_seg[None, :]) & (
        query_order[:, None] >= key_order[None, :]
    )
    return jnp.where(allowed[None, None], scores, -1e30)


def attend_forward(
    queries, key_all, value_all, query_seg, key_seg, query_order, key_order, block_rows, score_scale
):
    block_count = queries.shape[0] // block_rows

    def one_block(pieces):
        query_blk, seg_blk, order_blk = pieces
        scores = block_scores(
            query_blk, key_all, seg_blk, key_seg, order_blk, key_order, score_scale
        )
        highest = jnp.max(scores, axis=-1, keepdims=True)
        weights = jnp.exp(scores - highest)
        row_total = jnp.sum(weights, axis=-1, keepdims=True)
        probabilities = weights / row_total
        attended = jnp.einsum(
            "hgqk,khd->qhgd",
            probabilities.astype(jnp.bfloat16),
            value_all,
            preferred_element_type=jnp.float32,
        )
        return (attended, highest + jnp.log(row_total))

    stacked = (
        queries.reshape((block_count, block_rows) + queries.shape[1:]),
        query_seg.reshape(block_count, block_rows),
        query_order.reshape(block_count, block_rows),
    )
    attended, logsum = lax.map(one_block, stacked)
    return (attended.reshape(queries.shape), logsum)


def attend_backward(
    queries,
    key_all,
    value_all,
    grad_attended,
    logsum,
    query_seg,
    key_seg,
    query_order,
    key_order,
    block_rows,
    score_scale,
):
    block_count = queries.shape[0] // block_rows
    empty_grad = jnp.zeros(key_all.shape, jnp.float32)

    def one_block(carry, pieces):
        grad_key, grad_value = carry
        query_blk, grad_blk, logsum_blk, seg_blk, order_blk = pieces
        scores = block_scores(
            query_blk, key_all, seg_blk, key_seg, order_blk, key_order, score_scale
        )
        probabilities = jnp.exp(scores - logsum_blk)
        grad_probs = jnp.einsum(
            "qhgd,khd->hgqk", grad_blk, value_all, preferred_element_type=jnp.float32
        )
        row_delta = jnp.sum(probabilities * grad_probs, axis=-1, keepdims=True)
        grad_scores = (probabilities * (grad_probs - row_delta)).astype(jnp.bfloat16)
        grad_query = score_scale * jnp.einsum(
            "hgqk,khd->qhgd", grad_scores, key_all, preferred_element_type=jnp.float32
        )
        grad_key = grad_key + score_scale * jnp.einsum(
            "hgqk,qhgd->khd", grad_scores, query_blk, preferred_element_type=jnp.float32
        )
        grad_value = grad_value + jnp.einsum(
            "hgqk,qhgd->khd",
            probabilities.astype(jnp.bfloat16),
            grad_blk,
            preferred_element_type=jnp.float32,
        )
        return ((grad_key, grad_value), grad_query)

    stacked = (
        queries.reshape((block_count, block_rows) + queries.shape[1:]),
        grad_attended.reshape((block_count, block_rows) + grad_attended.shape[1:]),
        logsum,
        query_seg.reshape(block_count, block_rows),
        query_order.reshape(block_count, block_rows),
    )
    (grad_key, grad_value), grad_query = lax.scan(one_block, (empty_grad, empty_grad), stacked)
    return (grad_query.reshape(queries.shape), grad_key, grad_value)


def per_device_general(
    tokens,
    segments,
    positions,
    attn_gain,
    w_query,
    w_key,
    w_value,
    w_out,
    ffn_gain,
    w_gate,
    w_up,
    w_down,
    cotangent,
):
    token_count = tokens.shape[1]
    residual = tokens[0].astype(jnp.float32)
    seq_start = lax.axis_index("context") * token_count
    key_seg = segments[0]
    key_order = jnp.arange(key_seg.shape[0], dtype=jnp.int32)
    query_seg = lax.dynamic_slice_in_dim(key_seg, seq_start, token_count)
    query_order = seq_start + jnp.arange(token_count, dtype=jnp.int32)
    cos_table, sine_table = rotary(positions[0])
    block_rows = math.gcd(token_count, 512)
    score_scale = 1.0 / math.sqrt(HEAD)
    gain_one, query_w, key_w, value_w, out_w = (
        lax.all_gather(attn_gain, "fsdp", axis=0, tiled=True),
        lax.all_gather(w_query, "fsdp", axis=0, tiled=True),
        lax.all_gather(w_key, "fsdp", axis=0, tiled=True),
        lax.all_gather(w_value, "fsdp", axis=0, tiled=True),
        lax.all_gather(w_out, "fsdp", axis=0, tiled=True),
    )
    gain_two, gate_w, up_w, down_w = (
        lax.all_gather(ffn_gain, "fsdp", axis=0, tiled=True),
        lax.all_gather(w_gate, "fsdp", axis=0, tiled=True),
        lax.all_gather(w_up, "fsdp", axis=0, tiled=True),
        lax.all_gather(w_down, "fsdp", axis=0, tiled=True),
    )
    query_heads = query_w.shape[1] // HEAD
    kv_heads = key_w.shape[1] // HEAD
    group_size = query_heads // kv_heads
    inverse_one, normal_one = norm_forward(residual)
    normed_one = (normal_one * gain_one.astype(jnp.float32)).astype(jnp.bfloat16)
    query_raw = jnp.dot(normed_one, query_w, preferred_element_type=jnp.float32)
    key_raw = jnp.dot(normed_one, key_w, preferred_element_type=jnp.float32)
    value_raw = jnp.dot(normed_one, value_w, preferred_element_type=jnp.float32)
    queries = rotate(
        query_raw.reshape(token_count, query_heads, HEAD), cos_table, sine_table
    ).astype(jnp.bfloat16)
    queries = queries.reshape(token_count, kv_heads, group_size, HEAD)
    key_local = rotate(key_raw.reshape(token_count, kv_heads, HEAD), cos_table, sine_table).astype(
        jnp.bfloat16
    )
    value_local = value_raw.astype(jnp.bfloat16).reshape(token_count, kv_heads, HEAD)
    key_all, value_all = (
        lax.all_gather(key_local, "context", axis=0, tiled=True),
        lax.all_gather(value_local, "context", axis=0, tiled=True),
    )
    attended, logsum = attend_forward(
        queries,
        key_all,
        value_all,
        query_seg,
        key_seg,
        query_order,
        key_order,
        block_rows,
        score_scale,
    )
    attended_low = attended.reshape(token_count, query_heads * HEAD).astype(jnp.bfloat16)
    attn_part = jnp.dot(attended_low, out_w, preferred_element_type=jnp.float32)
    hidden = residual + lax.psum(attn_part, "tensor")
    inverse_two, normal_two = norm_forward(hidden)
    normed_two = (normal_two * gain_two.astype(jnp.float32)).astype(jnp.bfloat16)
    gate_proj = jnp.dot(normed_two, gate_w, preferred_element_type=jnp.float32)
    up_proj = jnp.dot(normed_two, up_w, preferred_element_type=jnp.float32)
    sigmoid_gate = jax.nn.sigmoid(gate_proj)
    silu_gate = gate_proj * sigmoid_gate
    activation = (silu_gate * up_proj).astype(jnp.bfloat16)
    ffn_part = jnp.dot(activation, down_w, preferred_element_type=jnp.float32)
    block_out = hidden + lax.psum(ffn_part.astype(jnp.bfloat16), "tensor").astype(jnp.float32)
    output = block_out.astype(jnp.bfloat16)[None]
    grad_rows = cotangent[0]
    term_down = contract_rows(activation, grad_rows)
    grad_act = contract_cols(grad_rows, down_w)
    grad_gate = (
        grad_act * up_proj * sigmoid_gate * (1.0 + gate_proj * (1.0 - sigmoid_gate))
    ).astype(jnp.bfloat16)
    grad_up = (grad_act * silu_gate).astype(jnp.bfloat16)
    term_gate = contract_rows(normed_two, grad_gate)
    term_up = contract_rows(normed_two, grad_up)
    grad_norm_two = contract_cols(grad_gate, gate_w) + contract_cols(grad_up, up_w)
    grad_norm_two = lax.psum(grad_norm_two, "tensor")
    term_gain_two = jnp.sum(grad_norm_two * normal_two, axis=0)
    grad_hidden = grad_rows.astype(jnp.float32) + norm_backward(
        grad_norm_two, gain_two.astype(jnp.float32), inverse_two, normal_two
    )
    hidden_low = grad_hidden.astype(jnp.bfloat16)
    term_out = contract_rows(attended_low, hidden_low)
    grad_attended = (
        contract_cols(hidden_low, out_w)
        .astype(jnp.bfloat16)
        .reshape(token_count, kv_heads, group_size, HEAD)
    )
    key_back, value_back = (key_all, value_all)
    grad_query, grad_key_all, grad_value_all = attend_backward(
        queries,
        key_back,
        value_back,
        grad_attended,
        logsum,
        query_seg,
        key_seg,
        query_order,
        key_order,
        block_rows,
        score_scale,
    )
    grad_key_rot, grad_value_rot = (
        lax.psum_scatter(grad_key_all, "context", scatter_dimension=0, tiled=True),
        lax.psum_scatter(grad_value_all, "context", scatter_dimension=0, tiled=True),
    )
    grad_query_low = unrotate(
        grad_query.reshape(token_count, query_heads, HEAD), cos_table, sine_table
    )
    grad_query_low = grad_query_low.reshape(token_count, query_heads * HEAD).astype(jnp.bfloat16)
    grad_key_low = (
        unrotate(grad_key_rot, cos_table, sine_table)
        .reshape(token_count, kv_heads * HEAD)
        .astype(jnp.bfloat16)
    )
    grad_value_low = grad_value_rot.reshape(token_count, kv_heads * HEAD).astype(jnp.bfloat16)
    term_query = contract_rows(normed_one, grad_query_low)
    term_key = contract_rows(normed_one, grad_key_low)
    term_value = contract_rows(normed_one, grad_value_low)
    grad_norm_one = (
        contract_cols(grad_query_low, query_w)
        + contract_cols(grad_key_low, key_w)
        + contract_cols(grad_value_low, value_w)
    )
    grad_norm_one = lax.psum(grad_norm_one, "tensor")
    term_gain_one = jnp.sum(grad_norm_one * normal_one, axis=0)
    grad_input = grad_hidden + norm_backward(
        grad_norm_one, gain_one.astype(jnp.float32), inverse_one, normal_one
    )
    summed = (
        lax.psum_scatter(term_gain_one, ("context", "fsdp"), scatter_dimension=0, tiled=True),
        lax.psum_scatter(term_query, ("context", "fsdp"), scatter_dimension=0, tiled=True),
        lax.psum_scatter(term_key, ("context", "fsdp"), scatter_dimension=0, tiled=True),
        lax.psum_scatter(term_value, ("context", "fsdp"), scatter_dimension=0, tiled=True),
        lax.psum_scatter(term_out, ("context", "fsdp"), scatter_dimension=0, tiled=True),
        lax.psum_scatter(term_gain_two, ("context", "fsdp"), scatter_dimension=0, tiled=True),
        lax.psum_scatter(term_gate, ("context", "fsdp"), scatter_dimension=0, tiled=True),
        lax.psum_scatter(term_up, ("context", "fsdp"), scatter_dimension=0, tiled=True),
        lax.psum_scatter(term_down, ("context", "fsdp"), scatter_dimension=0, tiled=True),
    )
    return (
        output,
        grad_input.astype(jnp.bfloat16)[None],
        summed[0],
        summed[1],
        summed[2],
        summed[3],
        summed[4],
        summed[5],
        summed[6],
        summed[7],
        summed[8],
    )


def low(values):
    return values.astype(jnp.bfloat16)


def wide(values):
    return values.astype(jnp.float32)


def matmul(left, right):
    return jnp.dot(left, right, preferred_element_type=jnp.float32)


def fence(*arrays):
    return lax.optimization_barrier(arrays)


def place_pair(mine, theirs, index, axis):
    first = index == 0
    return jnp.concatenate(
        [jnp.where(first, mine, theirs), jnp.where(first, theirs, mine)], axis=axis
    )


def cut(block, index, size, axis):
    return lax.dynamic_slice_in_dim(block, index * size, size, axis=axis)


def over_core(block):
    return lax.ppermute(block, "context", [(i, i ^ 1) for i in range(4)])


def over_y(block):
    return lax.ppermute(block, "context", [(i, i ^ 2) for i in range(4)])


def over_diagonal(block):
    return lax.ppermute(block, "context", [(i, i ^ 3) for i in range(4)])


def over_x(block):
    return lax.ppermute(block, "tensor", [(0, 1), (1, 0)])


def shift_z(block, step=1):
    return lax.ppermute(block, "fsdp", [(i, (i + step) % 4) for i in range(4)])


def gather_z(block):
    return lax.all_gather(block, "fsdp", axis=0, tiled=True)


def scatter_z(block):
    return lax.psum_scatter(block, "fsdp", scatter_dimension=0, tiled=True)


def gain_start(term):
    return term, over_x(term)


def gain_next(term, got, index, exchange, axis=0):
    term = term + got
    kept = lax.dynamic_index_in_dim(term, index, axis, keepdims=False)
    return kept, exchange(lax.dynamic_index_in_dim(term, 1 - index, axis, keepdims=False))


def flat(pieces):
    return [block for piece in pieces for block in piece]


def context_send(blocks, context_at):
    size = blocks.shape[0] // 4
    return (
        cut(blocks, context_at, size, 0),
        over_core(cut(blocks, context_at ^ 1, size, 0)),
        over_y(cut(blocks, context_at ^ 2, size, 0)),
        over_diagonal(cut(blocks, context_at ^ 3, size, 0)),
    )


def context_order(got, context_at):
    got = jnp.stack(got)
    return [lax.dynamic_index_in_dim(got, i ^ context_at, 0, keepdims=False) for i in range(4)]


def dot_dims(left, right, left_dim, right_dim):
    return lax.dot_general(
        left, right, (((left_dim,), (right_dim,)), ((), ())), preferred_element_type=jnp.float32
    )


def attend_kernel(
    scale, block, raw_ref, cos_ref, sine_ref, tag_ref, tag_row_ref, turned_ref, out_ref, sum_ref
):
    length = raw_ref.shape[0]
    heads = out_ref.shape[1] // HEAD

    def turn(rows, cols):
        part = raw_ref[rows, cols]
        return low(part * cos_ref[rows, :] + pltpu.roll(part, HEAD // 2, 1) * sine_ref[rows, :])

    everything = slice(0, length)
    key_cols = slice(heads * HEAD, (heads + 1) * HEAD)
    value_cols = slice((heads + 1) * HEAD, (heads + 2) * HEAD)
    keys = turn(everything, key_cols)
    values = low(raw_ref[:, value_cols])
    turned_ref[:, key_cols] = keys
    turned_ref[:, value_cols] = values
    for start in range(0, length, block):
        rows = slice(start, start + block)
        allowed = (tag_ref[rows, 0:1] == tag_row_ref[0:1, :]) & (
            tag_ref[rows, 1:2] >= tag_row_ref[1:2, :]
        )
        for head in range(heads):
            cols = slice(head * HEAD, (head + 1) * HEAD)
            queries = turn(rows, cols)
            turned_ref[rows, cols] = queries
            scores = jnp.where(allowed, dot_dims(queries, keys, 1, 1) * scale, -1e30)
            highest = jnp.max(scores, axis=-1, keepdims=True)
            weights = jnp.exp(scores - highest)
            row_total = jnp.sum(weights, axis=-1, keepdims=True)
            probabilities = low(weights * (1.0 / row_total))
            out_ref[rows, cols] = low(dot_dims(probabilities, values, 1, 0))
            sum_ref[rows, head : head + 1] = highest + jnp.log(row_total)


def attend_back_kernel(
    scale,
    block,
    turned_ref,
    grad_ref,
    sum_ref,
    cos_ref,
    sine_ref,
    tag_ref,
    tag_row_ref,
    out_ref,
    key_acc,
    value_acc,
):
    length = turned_ref.shape[0]
    heads = grad_ref.shape[1] // HEAD

    def turn_back(part, rows):
        return low(part * cos_ref[rows, :] - pltpu.roll(part, HEAD // 2, 1) * sine_ref[rows, :])

    key_cols = slice(heads * HEAD, (heads + 1) * HEAD)
    value_cols = slice((heads + 1) * HEAD, (heads + 2) * HEAD)
    keys, values = turned_ref[:, key_cols], turned_ref[:, value_cols]
    key_acc[...] = jnp.zeros_like(key_acc)
    value_acc[...] = jnp.zeros_like(value_acc)
    for start in range(0, length, block):
        rows = slice(start, start + block)
        allowed = (tag_ref[rows, 0:1] == tag_row_ref[0:1, :]) & (
            tag_ref[rows, 1:2] >= tag_row_ref[1:2, :]
        )
        for head in range(heads):
            cols = slice(head * HEAD, (head + 1) * HEAD)
            queries, grad = turned_ref[rows, cols], grad_ref[rows, cols]
            scores = jnp.where(allowed, dot_dims(queries, keys, 1, 1) * scale, -1e30)
            probabilities = jnp.exp(scores - sum_ref[rows, head : head + 1])
            grad_probs = dot_dims(grad, values, 1, 1)
            row_delta = jnp.sum(probabilities * grad_probs, axis=-1, keepdims=True)
            grad_scores = low(probabilities * (grad_probs - row_delta))
            out_ref[rows, cols] = turn_back(scale * dot_dims(grad_scores, keys, 1, 0), rows)
            key_acc[...] += dot_dims(grad_scores, queries, 0, 0)
            value_acc[...] += dot_dims(low(probabilities), grad, 0, 0)
    out_ref[:, key_cols] = turn_back(scale * key_acc[...], slice(0, length))
    out_ref[:, value_cols] = low(value_acc[...])


def feed_forward_kernel(*refs):
    tokens_refs, cotangent_refs, (gate_ref, up_ref, down_ref) = refs[:2], refs[2:4], refs[4:7]
    activation_ref, gate_grad_ref, up_grad_ref = refs[7:10]
    norm_refs, part_refs = refs[10:12], refs[12:14]
    size = tokens_refs[0].shape[0]
    for i in range(2):
        rows = slice(i * size, (i + 1) * size)
        gate_proj = dot_dims(tokens_refs[i][...], gate_ref[...], 1, 0)
        up_proj = dot_dims(tokens_refs[i][...], up_ref[...], 1, 0)
        sigmoid_gate = jax.nn.sigmoid(gate_proj)
        silu_gate = gate_proj * sigmoid_gate
        activation = low(silu_gate * up_proj)
        activation_ref[rows, :] = activation
        part_refs[i][...] = low(dot_dims(activation, down_ref[...], 1, 0))
        grad_act = dot_dims(cotangent_refs[i][...], down_ref[...], 1, 1)
        grad_gate = low(
            grad_act * up_proj * sigmoid_gate * (1.0 + gate_proj * (1.0 - sigmoid_gate))
        )
        grad_up = low(grad_act * silu_gate)
        gate_grad_ref[rows, :] = grad_gate
        up_grad_ref[rows, :] = grad_up
        norm_refs[i][...] = low(
            dot_dims(grad_gate, gate_ref[...], 1, 1) + dot_dims(grad_up, up_ref[...], 1, 1)
        )


def feed_forward_local(tokens, cotangents, gate_w, up_w, down_w):
    size, width = tokens[0].shape
    units = gate_w.shape[1]
    small = jax.ShapeDtypeStruct((2 * size, units), jnp.bfloat16)
    large = jax.ShapeDtypeStruct((size, width), jnp.bfloat16)
    return pl.pallas_call(
        feed_forward_kernel,
        out_shape=[small] * 3 + [large] * 4,
        compiler_params=pltpu.CompilerParams(vmem_limit_bytes=48 * 2**20),
        cost_estimate=NO_COST,
    )(*tokens, *cotangents, gate_w, up_w, down_w)


def weight_kernel(count, *refs):
    wide_refs, narrow_refs, (out_ref, acc_ref) = refs[:count], refs[count:-2], refs[-2:]
    size = wide_refs[0].shape[0]
    each = count // len(narrow_refs)
    transposed = out_ref.shape[1] == wide_refs[0].shape[1]
    for i in range(count):
        first = (i % each) * size
        narrow = narrow_refs[i // each][first : first + size, :]
        pair = (narrow, wide_refs[i][...]) if transposed else (wide_refs[i][...], narrow)
        term = dot_dims(*pair, 0, 0)
        if i == 0:
            acc_ref[...] = term
        else:
            acc_ref[...] += term
    out_ref[...] = low(acc_ref[...])


def weight_local(wides, narrows, transposed):
    size, width = wides[0].shape
    length, units = narrows[0].shape
    cols = width // 2
    tile = (units, cols) if transposed else (cols, units)
    return pl.pallas_call(
        functools.partial(weight_kernel, len(wides)),
        grid=(2,),
        in_specs=[pl.BlockSpec((size, cols), lambda i: (0, i))] * len(wides)
        + [pl.BlockSpec((length, units), lambda i: (0, 0))] * len(narrows),
        out_specs=pl.BlockSpec(tile, (lambda i: (0, i)) if transposed else (lambda i: (i, 0))),
        out_shape=jax.ShapeDtypeStruct(
            (units, width) if transposed else (width, units), jnp.bfloat16
        ),
        scratch_shapes=[pltpu.VMEM(tile, jnp.float32)],
        compiler_params=pltpu.CompilerParams(vmem_limit_bytes=48 * 2**20),
        cost_estimate=NO_COST,
    )(*wides, *narrows)


def attend_tables(places, seg, order):
    cos_table, sine_table = rotary(places)
    signs = jnp.where(jnp.arange(HEAD) < HEAD // 2, -1.0, 1.0)
    return cos_table, sine_table * signs, jnp.stack([seg, order], axis=1), jnp.stack([seg, order])


def attend_forward_local(raw, tables, heads, score_scale):
    length = raw.shape[0]
    return pl.pallas_call(
        functools.partial(attend_kernel, score_scale, math.gcd(length, 512)),
        out_shape=[
            jax.ShapeDtypeStruct(raw.shape, jnp.bfloat16),
            jax.ShapeDtypeStruct((length, heads * HEAD), jnp.bfloat16),
            jax.ShapeDtypeStruct((length, heads), jnp.float32),
        ],
        compiler_params=pltpu.CompilerParams(vmem_limit_bytes=48 * 2**20),
        cost_estimate=NO_COST,
    )(raw, *tables)


def attend_backward_local(turned, grad_attended, logsum, tables, heads, score_scale):
    length = turned.shape[0]
    return pl.pallas_call(
        functools.partial(attend_back_kernel, score_scale, math.gcd(length, 512)),
        out_shape=jax.ShapeDtypeStruct(turned.shape, jnp.bfloat16),
        scratch_shapes=[pltpu.VMEM((length, HEAD), jnp.float32)] * 2,
        compiler_params=pltpu.CompilerParams(vmem_limit_bytes=48 * 2**20),
        cost_estimate=NO_COST,
    )(turned, grad_attended, logsum, *tables)


def per_device_moved(
    tokens,
    segments,
    positions,
    attn_gain,
    w_query,
    w_key,
    w_value,
    w_out,
    ffn_gain,
    w_gate,
    w_up,
    w_down,
    cotangent,
):
    tensor_at, context_at, fsdp_at = (lax.axis_index(a) for a in ("tensor", "context", "fsdp"))
    y_at, core_at = context_at // 2, context_at % 2
    places = [(fsdp_at - r) % 4 for r in range(4)]
    width = tokens.shape[2]
    block_rows = tokens.shape[1]
    rows = block_rows // 2
    length = segments.shape[1]
    score_scale = 1.0 / math.sqrt(HEAD)
    shard = attn_gain.shape[0]
    head_cols = w_query.shape[1] // 4
    kv_cols = w_key.shape[1] // 4
    heads = head_cols // HEAD
    all_cols = head_cols + 2 * kv_cols
    unit_half = w_gate.shape[1] // 16
    units = 2 * unit_half

    half_width = width // 2

    def split_x(block):
        first, second = block[:rows], block[rows:]
        return jnp.concatenate(
            [
                jnp.where(tensor_at == 0, first, second),
                jnp.where(tensor_at == 0, second, first),
            ]
        )

    def spread_context(block):
        pair = jnp.concatenate([block, over_y(block)])
        return jnp.concatenate([pair, over_core(pair)])

    own_cotangent = split_x(cotangent[0])
    part = rows // PARTS
    gains = jnp.concatenate([attn_gain, ffn_gain]).reshape(-1, all_cols)
    gain_rows = gains.shape[0] // 2
    pieces = [
        jnp.concatenate(
            [
                cut(w_query, context_at, head_cols, 1),
                cut(w_key, context_at, kv_cols, 1),
                cut(w_value, context_at, kv_cols, 1),
            ],
            axis=1,
        ),
        cut(w_out, context_at, all_cols, 1),
        jnp.pad(gains, ((0, 16 - gains.shape[0]), (0, 0))),
    ]
    packed = lax.all_gather(jnp.concatenate(pieces), "fsdp", axis=0, tiled=False)
    own_tokens = split_x(tokens[0])
    all_tokens = spread_context(own_tokens)
    all_places = spread_context(split_x(positions[0]))

    def unit_weights(place):
        first = ((place * 2 + core_at) * 2 + y_at) * unit_half
        return jnp.concatenate(
            [
                lax.dynamic_slice_in_dim(w_gate, first, unit_half, axis=1),
                lax.dynamic_slice_in_dim(w_up, first, unit_half, axis=1),
            ],
            axis=1,
        )

    unit_own = unit_weights(fsdp_at)
    unit_out = [unit_weights((fsdp_at + step) % 4) for step in (1, 2, 3)]
    down_w = cut(w_down, core_at, units, 0)

    def flip(block, axis, index):
        return jnp.where(index == 0, block, jnp.flip(block, axis))

    def relative(block):
        block = block.reshape(2, 2, 2, rows)
        block = flip(flip(flip(block, 0, y_at), 1, core_at), 2, tensor_at)
        return jnp.swapaxes(block, 0, 1).reshape(length)

    order = relative(jnp.arange(length, dtype=jnp.int32))
    tables = attend_tables(all_places, relative(segments[0]), order)
    residual = wide(all_tokens)
    inverse_one = lax.rsqrt(jnp.mean(residual * residual, axis=-1, keepdims=True) + norm_epsilon)
    all_tokens, unit_own = fence(all_tokens, unit_own)
    packed, unit_own_given, all_tokens, inverse_one, own_cotangent, down_w, *rest = fence(
        packed, over_y(unit_own), all_tokens, inverse_one, own_cotangent, down_w, *unit_out, *tables
    )
    unit_out, tables = rest[:3], rest[3:]

    at = [0]
    for piece in pieces:
        at.append(at[-1] + piece.shape[0])
    attn_w = packed[:, : at[1]].reshape(width, all_cols)
    out_part = packed[:, at[1] : at[2]].reshape(4 * w_out.shape[0], all_cols)
    gain_one = wide(packed[:, at[2] : at[2] + gain_rows].reshape(width))
    gain_two = wide(packed[:, at[2] + gain_rows : at[2] + 2 * gain_rows].reshape(width))
    cot_own = [gather_z(own_cotangent[:part]), None]
    unit_got = [shift_z(unit_out[0], 1), unit_out[1], shift_z(unit_out[2], 3)]
    out_got = context_send(out_part, context_at)
    normed_one = low(wide(all_tokens) * inverse_one * gain_one)
    turned, attended, logsum = attend_forward_local(
        matmul(normed_one, attn_w), tables, heads, score_scale
    )
    attended, cot_own[0], cot_late, *rest = fence(
        attended, cot_own[0], own_cotangent[part:rows], *unit_got, *out_got
    )
    unit_got, out_got = rest[:3], rest[3:]

    unit_got[1] = shift_z(unit_got[1], 2)
    cot_own[1] = gather_z(cot_late)
    cot_x = [over_x(cot_own[0])]
    out_w = jnp.concatenate(context_order(out_got, context_at), axis=1)
    part_shape = (2, 2, rows, width)

    def plane_first(theirs, mine):
        return low(wide(mine) + wide(over_core(theirs)))

    def plane_second(mine):
        left, right = mine[..., :half_width], mine[..., half_width:]
        return left[:, 0], over_x(left[:, 1]), right[0], over_y(right[1])

    def plane_third(left, left_got, right, right_got):
        left = low(wide(left) + wide(left_got))
        right = low(wide(right) + wide(right_got))
        return left[0], over_y(left[1]), right[0], over_x(right[1])

    def plane_last(left, left_got, right, right_got):
        return jnp.concatenate(
            [wide(left) + wide(left_got), wide(right) + wide(right_got)], axis=-1
        )

    theirs = low(matmul(attended[length // 2 :], out_w)).reshape(part_shape)
    mine = low(matmul(attended[: length // 2], out_w)).reshape(part_shape)
    (mine,) = fence(plane_first(theirs, mine))
    parts = fence(*plane_second(mine))
    parts = fence(*plane_third(*parts), unit_got[1], cot_x[0], cot_own[1])
    unit_got[1], cot_x[0], cot_own[1] = parts[4:]
    own_residual = wide(own_tokens[:rows])
    hidden = own_residual + plane_last(*parts[:4])
    inverse_two, normal_two = norm_forward(hidden)
    normed_two = low(normal_two * gain_two)
    normed_two, cot_own[1], cot_own[0], cot_x[0], unit_got[0], unit_got[1], unit_got[2] = fence(
        normed_two, cot_own[1], cot_own[0], cot_x[0], *unit_got
    )

    normed_own = [gather_z(normed_two[:part])]
    unit_given = [over_y(jnp.concatenate([unit_got[0], unit_got[2]]))]
    cot_x.append(over_x(cot_own[1]))
    cot_core = [[over_core(cot_own[0]), over_core(cot_x[0])]]
    own_units = jnp.zeros((width, units), jnp.bfloat16)
    other_units = lax.dynamic_update_slice_in_dim(own_units, unit_own_given, places[0] * shard, 0)
    for r, block in enumerate([unit_own] + list(unit_got)):
        own_units = lax.dynamic_update_slice_in_dim(own_units, block, places[r] * shard, 0)
    (
        normed_own[0],
        cot_x[1],
        later,
        cot_own[1],
        own_units,
        other_units,
        unit_given[0],
        unit_got[1],
        *cot_core[0],
    ) = fence(
        normed_own[0],
        cot_x[1],
        normed_two[part:],
        cot_own[1],
        own_units,
        other_units,
        unit_given[0],
        unit_got[1],
        *cot_core[0],
    )

    normed_own.append(gather_z(later))
    normed_x = [over_x(normed_own[0])]
    unit_given.append(over_y(unit_got[1]))
    cot_core.append([over_core(cot_own[1]), over_core(cot_x[1])])
    for block, place in (
        (unit_given[0][:shard], places[1]),
        (unit_given[0][shard:], places[3]),
        (unit_given[1], places[2]),
    ):
        other_units = lax.dynamic_update_slice_in_dim(other_units, block, place * shard, 0)
    normed_core = over_core(normed_own[0])
    (
        normed_own[1],
        normed_x[0],
        normed_core,
        own_units,
        other_units,
        cot_own[1],
        cot_x[1],
        *cot_core[1],
    ) = fence(
        normed_own[1],
        normed_x[0],
        normed_core,
        own_units,
        other_units,
        cot_own[1],
        cot_x[1],
        *cot_core[1],
    )
    gate_w = place_pair(own_units[:, :unit_half], other_units[:, :unit_half], y_at, 1)
    up_w = place_pair(own_units[:, unit_half:], other_units[:, unit_half:], y_at, 1)

    def total(mine, theirs):
        return low(wide(mine) + wide(theirs))

    def piece_of(i, k, normed):
        cot = ((cot_own, cot_x)[k][i], cot_core[i][k])
        small = feed_forward_local(normed, cot, gate_w, up_w, down_w)
        return list(normed) + list(cot) + list(small)

    def send_y(term):
        return over_y(cut(term, 1 - y_at, half_width, 0))

    gate_w, up_w, normed_x[0], normed_own[1], normed_x_core = fence(
        gate_w, up_w, normed_x[0], normed_own[1], over_core(normed_x[0])
    )
    kept = [None] * 4
    normed_x.append(over_x(normed_own[1]))
    kept[1] = piece_of(0, 1, (normed_x[0], normed_x_core))
    kept[0] = piece_of(0, 0, (normed_own[0], normed_core))
    normed_x[1], normed_own[1], *rest = fence(normed_x[1], normed_own[1], *kept[1], *kept[0])
    kept[1], kept[0] = rest[:11], rest[11:]
    give_core, keep_core, normed_x_core, normed_late, *rest = fence(
        over_core(kept[1][8]),
        over_core(kept[0][8]),
        over_core(normed_x[1]),
        over_core(normed_own[1]),
        normed_x[1],
        normed_own[1],
        kept[1][7],
        kept[0][7],
    )
    normed_x[1], normed_own[1], give, keep = rest
    keeps = [total(keep, keep_core)]
    give_x = [over_x(total(give, give_core))]
    kept[3] = piece_of(1, 1, (normed_x[1], normed_x_core))
    give_x[0], keeps[0], normed_late, normed_own[1], *kept[3] = fence(
        give_x[0], keeps[0], normed_late, normed_own[1], *kept[3]
    )
    give_core, norm_term, give, normed_late, normed_own[1] = fence(
        over_core(kept[3][8]), total(keeps[0], give_x[0]), kept[3][7], normed_late, normed_own[1]
    )

    norm_two = [scatter_z(norm_term)]
    give_x.append(over_x(total(give, give_core)))
    kept[2] = piece_of(1, 0, (normed_own[1], normed_late))

    def weight_sum(wide_at, narrow_at, transposed=False):
        return weight_local(
            flat(piece[wide_at : wide_at + 2] for piece in kept),
            [piece[narrow_at] for piece in kept],
            transposed,
        )

    term_gate = weight_sum(0, 5)
    give_x[1], norm_two[0], term_gate, *rest = fence(
        give_x[1], norm_two[0], term_gate, *flat(kept)
    )
    kept = [rest[11 * i : 11 * i + 11] for i in range(4)]
    keep_core, keep, give_x[1], term_gate, out_keep, out_keep_core, out_give, out_give_core, *rest = fence(
        over_core(kept[2][8]),
        kept[2][7],
        give_x[1],
        term_gate,
        kept[0][9],
        over_core(kept[0][10]),
        kept[1][9],
        over_core(kept[1][10]),
        *flat(kept),
    )
    kept = [rest[11 * i : 11 * i + 11] for i in range(4)]

    def unit_sum(term, given):
        term = low(wide(cut(term, y_at, half_width, 0)) + wide(given))
        return cut(term, core_at, half_width // 2, 0), over_core(
            cut(term, 1 - core_at, half_width // 2, 0)
        )

    def to_owners(term):
        return [cut(term, fsdp_at, width // 16, 0)] + [
            shift_z(cut(term, (fsdp_at + step) % 4, width // 16, 0), step) for step in (1, 2, 3)
        ]

    norm_two.append(scatter_z(low(wide(keep) + wide(keep_core) + wide(give_x[1]))))
    gate_given = send_y(term_gate)
    out_x = [over_x(total(out_give, out_give_core))]
    out_first = total(out_keep, out_keep_core)
    term_up = weight_sum(0, 6)
    term_down = weight_sum(2, 4, True)
    norm_two[1], gate_given, out_x[0], term_up, term_down, *rest = fence(
        norm_two[1],
        gate_given,
        out_x[0],
        term_up,
        term_down,
        out_first,
        *kept[2][9:],
        *kept[3][9:],
    )
    out_first, parts_late = rest[0], [rest[1:3], rest[3:5]]

    grad_norm_two = wide(jnp.concatenate(norm_two))
    grad_hidden = wide(own_cotangent[:rows]) + norm_backward(
        grad_norm_two, gain_two, inverse_two, normal_two
    )
    hidden_low = low(grad_hidden)
    left, right = hidden_low[:, :half_width], hidden_low[:, half_width:]
    gate_pair = unit_sum(term_gate, gate_given)
    def gain_send(term):
        term = term.reshape(2, 2, 4, -1)
        parts = [
            lax.dynamic_index_in_dim(term, (fsdp_at + step) % 4, 2, keepdims=False)
            for step in range(4)
        ]
        return parts[:1] + [shift_z(parts[step], step) for step in (1, 2, 3)]

    gain_two_all = gain_send(jnp.sum(grad_norm_two * normal_two, axis=0))
    left, left_got, right, right_got, *rest = fence(
        left, over_x(left), right, over_y(right), *gate_pair, *gain_two_all
    )
    gate_pair, gain_two_sum = rest[:2], gain_start(sum(rest[2:]))
    gate_term = place_pair(*gate_pair, core_at, 1)
    ffn_out = [scatter_z(low(wide(out_first) + wide(out_x[0])))]
    left = jnp.stack([left, left_got])
    right = jnp.stack([right, right_got])
    out_last = flat((first, over_core(second)) for first, second in parts_late)
    left, left_got, right, right_got, gate_term, *rest = fence(
        left, over_y(left), right, over_x(right), gate_term, *gain_two_sum, *out_last
    )
    gain_two_sum, out_last = rest[:2], [total(*rest[2:4]), total(*rest[4:])]
    gain_two_sum = gain_next(*gain_two_sum, core_at, over_core, 1)
    mine = jnp.concatenate(
        [jnp.stack([left, left_got]), jnp.stack([right, right_got], axis=1)], axis=-1
    )
    mine, theirs, gate_term, ffn_out[0], term_up, *rest = fence(
        mine, over_core(mine), gate_term, ffn_out[0], term_up, *gain_two_sum, *out_last
    )
    gain_two_sum, out_last = rest[:2], rest[2:]

    hidden_low = jnp.stack([mine, theirs]).reshape(length, width)
    gate_sent = to_owners(gate_term)
    owned_out = scatter_z(low(contract_rows(attended, hidden_low)))
    up_given = send_y(term_up)
    out_x.append(over_x(out_last[1]))
    grad_attended = low(contract_cols(hidden_low, out_w))
    grad_heads = attend_backward_local(turned, grad_attended, logsum, tables, heads, score_scale)
    gain_two_sum = gain_next(*gain_two_sum, y_at, over_y)
    grad_heads, hidden_low, up_given, out_x[1], *rest = fence(
        grad_heads, hidden_low, up_given, out_x[1], *gate_sent, *gain_two_sum
    )
    gate_sent, gain_two_sum = rest[:4], rest[4:]
    grad_ffn_gain = gain_two_sum[0] + gain_two_sum[1]

    theirs = low(contract_cols(grad_heads[length // 2 :], attn_w)).reshape(part_shape)
    theirs = over_core(theirs)
    mine = low(contract_cols(grad_heads[: length // 2], attn_w)).reshape(part_shape)
    term_heads = contract_rows(normed_one, grad_heads)
    gain_term = jnp.sum(term_heads * wide(attn_w), axis=1) / gain_one
    term_heads = low(term_heads).reshape(4, 4, width // 16, all_cols).swapaxes(0, 1)
    mine, theirs, term_heads, gain_term, owned_out, term_up, up_given, out_x[1], *gate_sent = fence(
        mine,
        theirs,
        term_heads.reshape(width, all_cols),
        gain_term,
        owned_out,
        term_up,
        up_given,
        out_x[1],
        *gate_sent,
    )
    up_pair = unit_sum(term_up, up_given)
    owned_heads = scatter_z(term_heads)
    gain_one_all = gain_send(gain_term)
    parts = fence(*plane_second(total(mine, theirs)), *gain_one_all, *up_pair)
    gain_one_sum = gain_start(sum(parts[4:8]))
    grad_w_out = wide(owned_out)
    up_term = place_pair(*parts[8:], core_at, 1)
    parts = fence(*plane_third(*parts[:4]), *gain_one_sum, up_term, term_down, *out_last)
    grad_norm_one = plane_last(*parts[:4])
    gain_one_sum = gain_next(*parts[4:6], core_at, over_core, 1)
    up_term, term_down = parts[6:8]
    out_last = parts[8:]
    normal_one = own_residual * inverse_one[:rows]
    grad_input = low(
        grad_hidden + norm_backward(grad_norm_one, gain_one, inverse_one[:rows], normal_one)
    )

    out_term = low(wide(out_last[0]) + wide(out_x[1]))
    down_cols = [cut(term_down, i, half_width, 1) for i in (y_at, 1 - y_at)]
    down_given = over_y(down_cols[1])
    grad_input_x = over_x(grad_input)
    down_given, grad_input, grad_input_x, up_term, *gain_one_sum = fence(
        down_given, grad_input, grad_input_x, up_term, *gain_one_sum
    )
    grad_tokens = place_pair(grad_input, grad_input_x, tensor_at, 0)
    down_sum = low(wide(down_cols[0]) + wide(down_given))
    quarter = half_width // 2
    down_own, down_core, up_term, out_term, owned_heads = fence(
        cut(down_sum, core_at, quarter, 1),
        over_core(cut(down_sum, 1 - core_at, quarter, 1)),
        up_term,
        out_term,
        owned_heads,
    )
    ffn_out.append(scatter_z(out_term))

    down_blocks = place_pair(down_own, down_core, core_at, 0)
    down_got = [cut(down_blocks, fsdp_at, unit_half, 0)] + [
        shift_z(cut(down_blocks, (fsdp_at + step) % 4, unit_half, 0), step) for step in (1, 2, 3)
    ]
    heads_got = context_send(owned_heads, context_at)
    gain_one_sum = gain_next(*gain_one_sum, y_at, over_y)
    up_term, ffn_out[1], *rest = fence(
        up_term, ffn_out[1], *down_got, *heads_got, *gain_one_sum
    )
    down_got, heads_got = rest[:4], rest[4:8]
    grad_attn_gain = rest[8] + rest[9]
    up_sent = to_owners(up_term)
    block_out = low(hidden + wide(jnp.concatenate(ffn_out)))
    output = place_pair(block_out, over_x(block_out), tensor_at, 0)
    got = context_order(heads_got, context_at)
    grad_w_query = wide(jnp.concatenate([block[:, :head_cols] for block in got], axis=1))
    grad_w_key = wide(
        jnp.concatenate([block[:, head_cols : head_cols + kv_cols] for block in got], axis=1)
    )
    grad_w_value = wide(jnp.concatenate([block[:, head_cols + kv_cols :] for block in got], axis=1))
    unit_owned = []
    for got in (gate_sent, up_sent):
        owned = jnp.zeros((width // 16, 8 * units), jnp.float32)
        for r in range(4):
            owned = lax.dynamic_update_slice_in_dim(owned, wide(got[r]), places[r] * 2 * units, 1)
        unit_owned.append(owned)
    grad_w_gate, grad_w_up = unit_owned
    down_stack = jnp.stack(down_got)
    down_blocks = jnp.concatenate(
        [
            lax.dynamic_index_in_dim(down_stack, (fsdp_at - i) % 4, 0, keepdims=False)
            for i in range(4)
        ]
    )
    got = context_order(context_send(down_blocks, context_at), context_at)
    grad_w_down = wide(jnp.concatenate(got, axis=1))
    return (
        output[None],
        grad_tokens[None],
        grad_attn_gain,
        grad_w_query,
        grad_w_key,
        grad_w_value,
        grad_w_out,
        grad_ffn_gain,
        grad_w_gate,
        grad_w_up,
        grad_w_down,
    )


def solution(mesh):
    sizes = tuple(mesh.shape[a] for a in ("tensor", "context", "fsdp"))
    return jax.shard_map(
        per_device_moved if sizes == (2, 4, 4) else per_device_general,
        mesh=mesh,
        in_specs=(
            P("fsdp", "context", None),
            P("fsdp", None),
            P("fsdp", "context"),
            P("fsdp"),
            P("fsdp", "tensor"),
            P("fsdp", "tensor"),
            P("fsdp", "tensor"),
            P(("tensor", "fsdp"), None),
            P("fsdp"),
            P("fsdp", "tensor"),
            P("fsdp", "tensor"),
            P(("tensor", "fsdp"), None),
            P("fsdp", "context", None),
        ),
        out_specs=(
            P("fsdp", "context", None),
            P("fsdp", "context", None),
            P(("context", "fsdp")),
            P(("context", "fsdp"), "tensor"),
            P(("context", "fsdp"), "tensor"),
            P(("context", "fsdp"), "tensor"),
            P(("tensor", "context", "fsdp"), None),
            P(("context", "fsdp")),
            P(("context", "fsdp"), "tensor"),
            P(("context", "fsdp"), "tensor"),
            P(("tensor", "context", "fsdp"), None),
        ),
        check_vma=False,
    )
```
